128 devices in a mesh: prow: 16 (over x, z), pcol: 8 (over y, core).
Axes of the slice: x: 4, y: 4, z: 4, core: 2. Of those that a mesh axis runs over, the one named last changes fastest.
Arguments:
- ancestor_blocks: int32 [3, 24], replicated, may hold values from -1 to 31, as said below
- root_inverse: bfloat16 [8192, 8192], P('prow', 'pcol'), may hold values from -4.5 to 4.5, as said below
- factor_rows: bfloat16 [3, 6144, 2048], P(None, 'pcol', 'prow'), may hold values from -0.078125 to 0.078125
- diag_inverse: float32 [3, 2048], P(None, 'prow'), may hold values from 0.5 to 2
Outputs:
- inverse_diagonal: float32 [3, 2048], P(None, 'prow')
The draws below stay inside these ranges and needn't reach their ends.
Inputs may be any that keep to these rules, and one draw needn't show every extreme that they name: `ancestor_blocks`: row c lists distinct root block numbers in rising order, then -1 in the remaining slots; each child lists 24 // 2 to 24 blocks. root_inverse is exactly symmetric.
All inputs are finite; a program needn't handle non-finite values.
Results may differ from the reference program's by a relative error of at most 0.0018.
Values may be sent and summed in bfloat16 or wider, within the bound.
A program may use at most 128 MiB of HBM per device.

```python
import math
import jax
import jax.numpy as jnp
from jax import lax

ROOT = 8192
WIDTH = 2048
MAX_ANC = 24
CHILDREN = 3
ROOT_BLOCKS = 32
AROWS = 6144


def draw_ancestor_blocks(key, part):
    key = jax.random.fold_in(key, 11)
    first_key, second_key, third_key = jax.random.split(key, 3)
    counts = jax.random.randint(first_key, (CHILDREN,), MAX_ANC // 2, MAX_ANC + 1)
    widest = jax.random.randint(second_key, (), 0, CHILDREN)
    counts = jnp.where(jnp.arange(CHILDREN) == widest, MAX_ANC, counts)
    child_keys = jax.random.split(third_key, CHILDREN)
    orders = jax.vmap(lambda k: jax.random.permutation(k, ROOT_BLOCKS))(child_keys)
    chosen = orders[:, :MAX_ANC]
    slots = jnp.arange(MAX_ANC)
    marked = jnp.where(slots[None, :] < counts[:, None], chosen, ROOT_BLOCKS)
    ordered = jnp.sort(marked, axis=1)
    return jnp.where(ordered == ROOT_BLOCKS, -1, ordered).astype(jnp.int32)


def draw_root_inverse(key, part):
    key = jax.random.fold_in(key, 23)
    noise_key, diag_key = jax.random.split(key)
    noise = jnp.clip(jax.random.normal(noise_key, (ROOT, ROOT), jnp.float32), -5.0, 5.0)
    noise = noise * 0.3
    symmetric = (noise + noise.T) * 0.70710678
    diagonal = jnp.exp(jax.random.uniform(diag_key, (ROOT,), jnp.float32, 0.0, 0.69314718))
    eye_mask = jnp.arange(ROOT)[:, None] == jnp.arange(ROOT)[None, :]
    whole = jnp.where(eye_mask, diagonal[:, None] + symmetric, symmetric)
    return whole.astype(jnp.bfloat16)


def block_scale(own_key, shape, pieces, least, high):
    loudness, own = 1.0, jax.random.fold_in(own_key, 6)
    for axis_at, blocks in pieces:
        draws = jnp.exp(jax.random.uniform(jax.random.fold_in(own, axis_at), (blocks,), jnp.float32, least / len(pieces), high / len(pieces)))
        loudness = loudness * jnp.repeat(draws, shape[axis_at] // blocks).reshape([-1 if axis == axis_at else 1 for axis in range(len(shape))])
    return loudness


def centred(own_key, dims, spread, most, cuts=(), kind=jnp.bfloat16):
    result = jax.random.normal(own_key, dims, jnp.float32) * spread
    if len(cuts) > 0:
        result = block_scale(own_key, dims, cuts, -0.22, 0.18) * result
    return jnp.clip(result, min=-most, max=most).astype(kind)


def setup_inputs(seed: int = 0) -> dict:
    seeds = jax.random.split(jax.random.key(seed), 5)
    return {
        "ancestor_blocks": draw_ancestor_blocks(jax.random.fold_in(seeds[4], 71), 0),
        "root_inverse": draw_root_inverse(jax.random.fold_in(seeds[4], 71), 0),
        "factor_rows": centred(seeds[2], (CHILDREN, AROWS, WIDTH), AROWS ** -0.5, 0.078125, ((1, 8), (2, 16))),
        "diag_inverse": jnp.clip(jnp.exp(math.log(2.0) - 1.3862944 * jax.random.uniform(seeds[3], (CHILDREN, WIDTH), jnp.float32) ** block_scale(seeds[3], (CHILDREN, WIDTH), ((1, 16),), -0.2, 0.2)), 0.5, 2.0),
    }


def place_rows(blocks, rows):
    select = (blocks[:, None] == jnp.arange(ROOT_BLOCKS, dtype=jnp.int32)[None, :]).astype(jnp.float32)
    flat = rows.astype(jnp.float32).reshape(MAX_ANC, -1)
    placed = jnp.dot(select.T, flat, precision=lax.Precision.HIGHEST)
    return placed.astype(jnp.bfloat16).reshape(ROOT, WIDTH)


def reference(ancestor_blocks, root_inverse, factor_rows, diag_inverse):
    results = []
    for child in range(CHILDREN):
        placed = place_rows(ancestor_blocks[child], factor_rows[child])
        coupled = jnp.dot(root_inverse, placed, preferred_element_type=jnp.float32)
        total = jnp.sum(placed.astype(jnp.float32) * coupled, axis=0)
        results.append(diag_inverse[child] + total)
    return jnp.stack(results, axis=0)
```

```python
import jax
import jax.numpy as jnp
from jax import lax
from jax.experimental import pallas as pl
from jax.experimental.pallas import tpu as pltpu
from jax.sharding import PartitionSpec as P

MESH = pl.DeviceIdType.MESH
BLK = 256
CHILDREN = 3
ROOT_BLOCKS = 32
MAX_ANC = 24
Z_FIRST = (1, 2, 2)
FAR_UP = (1, 1, 0)
SOURCES = ((0, 0), (0, 1), (1, 0), (3, 0), (1, 1), (3, 1), (2, 0), (2, 1))
UNITS = 2 * len(SOURCES)
COPIES = 96


def pick(index, values):
    out = jnp.int32(values[0])
    for at, value in enumerate(values[1:], 1):
        out = jnp.where(index == at, jnp.int32(value), out)
    return out


def kernel(
    anc,
    root,
    rows,
    out,
    pb0,
    pb1,
    pb2,
    rb,
    ext,
    pk0,
    pk1,
    pk2,
    acc,
    part,
    red,
    slot_of,
    listed,
    unit_row,
    unit_win,
    local_sem,
    send_sem,
    recv_sem,
    ext_send,
    ext_recv,
    red_send,
    red_recv,
):
    pb, pk = (pb0, pb1, pb2), (pk0, pk1, pk2)
    p, q = lax.axis_index("prow"), lax.axis_index("pcol")
    x, z = p // 4, p % 4
    y, core = q // 2, q % 2
    zp = z + 1 - 2 * (z % 2)
    zq = (z + 3 + 2 * (z % 2)) % 4
    up, down, far = (y + 1) % 4, (y + 3) % 4, (y + 2) % 4

    def device(px, py, pz, pc):
        return (px * 4 + pz, py * 2 + pc)

    d_z = device(x, y, zp, core)
    d_yu, d_yd = device(x, up, z, core), device(x, down, z, core)
    d_zq = device(x, y, zq, core)
    d_xu, d_xd = device((x + 1) % 4, y, z, core), device((x + 3) % 4, y, z, core)
    d_core = device(x, y, z, 1 - core)

    def window(px, pz, t):
        diagonal = jnp.logical_and(px == y, pz // 2 == core)
        second = pz - 2 * core
        below = px * 4 + pz < 2 * q
        plain = 1 + 2 * jnp.where(below, t, 1 - t)
        special = jnp.where(second == 0, 1, 2) if t == 0 else jnp.where(second == 0, 3, 0)
        return jnp.where(diagonal, special, plain).astype(jnp.int32)

    own_diag = jnp.logical_and(x == y, z // 2 == core)
    z_ext = jnp.where(z // 2 == core, z, zq)
    ext_key = 1 + (z_ext - 2 * core)
    ext_row = 2 * (4 * y + z_ext) + 1

    local = []
    for c in range(CHILDREN):
        local.append(
            pltpu.make_async_copy(
                rows.at[c], pb[c].at[0, y, pl.ds(core * 3, 3)], local_sem.at[c]
            )
        )
    for t in range(2):
        win = window(x, z, t)
        for h, values in enumerate(((3, 0, 2, 1), (0, 2, 1, 3))):
            column = pl.multiple_of(pick(win, values) * BLK, BLK)
            local.append(
                pltpu.make_async_copy(
                    root.at[pl.ds(t * BLK, BLK), pl.ds(column, BLK)],
                    rb.at[t, :, pl.ds(h * BLK, BLK)],
                    local_sem.at[3 + 2 * t + h],
                )
            )
    ext_column = pl.multiple_of(jnp.where(z - 2 * core == 1, 2 * BLK, 0), BLK)
    local_ext = pltpu.make_async_copy(
        root.at[pl.ds(BLK, BLK), pl.ds(ext_column, BLK)], ext, local_sem.at[7]
    )
    for copy in local:
        copy.start()

    @pl.when(own_diag)
    def _():
        local_ext.start()

    group = [(dy, dc, dz) for dy in range(4) for dc in range(2) for dz in range(2)][1:]

    def member(dy, dc, dz):
        return device(x, (y + dy) % 4, zp if dz else z, 1 - core if dc else core)

    partners = [member(*g) for g in group] + [d_zq, d_xu, d_xd]
    barrier = pltpu.get_barrier_semaphore()
    for partner in partners:
        pl.semaphore_signal(barrier, inc=1, device_id=partner, device_id_type=MESH)
    for copy in local:
        copy.wait()

    @pl.when(own_diag)
    def _():
        local_ext.wait()
        for t in range(2):
            rb[t, :, 0:BLK] = rb[t, :, 0:BLK] * jnp.bfloat16(0.5)

    pl.semaphore_wait(barrier, len(partners))

    sent = []

    def send(src, dst, target):
        n = len(sent)
        copy = pltpu.make_async_remote_copy(
            src_ref=src,
            dst_ref=dst,
            send_sem=send_sem.at[n],
            recv_sem=recv_sem.at[n],
            device_id=target,
            device_id_type=MESH,
        )
        copy.start()
        sent.append(copy)
        return copy

    def slots(c, zz, py, lo, hi):
        return pb[c].at[zz, py, pl.ds(core * 3 + lo, hi - lo)]

    def unit(dx, zr, t):
        return rb.at[2 * SOURCES.index((dx, zr)) + t]

    def p_a(c):
        return send(slots(c, 0, y, 0, 3), slots(c, 1, y, 0, 3), d_z)

    def p_b(c):
        own = slots(c, 0, y, 0, 3)
        return send(own, own, d_yu), send(own, own, d_yd)

    def p_c(c):
        ref = slots(c, 1, y, 0, Z_FIRST[c])
        return send(ref, ref, d_yu), send(ref, ref, d_yd)

    def p_d_up(c):
        ref = slots(c, 0, down, 0, Z_FIRST[c] + FAR_UP[c])
        return send(ref, ref, d_yu)

    def p_d_down(c):
        if Z_FIRST[c] + FAR_UP[c] == 3:
            return None
        ref = slots(c, 0, up, Z_FIRST[c] + FAR_UP[c], 3)
        return send(ref, ref, d_yd)

    def p_d_other(c):
        ref = slots(c, 1, up, 0, Z_FIRST[c])
        return send(ref, ref, d_yd)

    def p_e(c, py):
        return send(slots(c, 0, py, Z_FIRST[c], 3), slots(c, 1, py, Z_FIRST[c], 3), d_z)

    def p_core(c, zz, py, lo, hi):
        ref = slots(c, zz, py, lo, hi)
        return send(ref, ref, d_core)

    def p_core_all(c):
        ref = pb[c].at[:, :, pl.ds(core * 3, 3)]
        return send(ref, ref, d_core)

    a, b, cc, du, dd, do, e = {}, {}, {}, {}, {}, {}, {}
    kids = []
    a[0] = p_a(0)
    b[0] = p_b(0)
    r_a0 = send(unit(0, 0, 0), unit(0, 1, 0), d_zq)
    r_b1 = send(unit(0, 0, 1), unit(3, 0, 1), d_xu), send(unit(0, 0, 1), unit(1, 0, 1), d_xd)
    r_a1 = send(unit(0, 0, 1), unit(0, 1, 1), d_zq)
    r_b0 = send(unit(0, 0, 0), unit(3, 0, 0), d_xu), send(unit(0, 0, 0), unit(1, 0, 0), d_xd)
    a[1] = p_a(1)
    b[1] = p_b(1)

    ext_is_mine = z_ext == z
    dx_ext = (x - y + 4) % 4

    def ext_copy(n, target):
        return pltpu.make_async_remote_copy(
            src_ref=ext,
            dst_ref=ext,
            send_sem=ext_send.at[n],
            recv_sem=ext_recv,
            device_id=target,
            device_id_type=MESH,
        )

    to_zq, to_xu, to_xd = ext_copy(0, d_zq), ext_copy(1, d_xu), ext_copy(2, d_xd)
    goes_zq = ext_is_mine
    goes_xu = jnp.logical_and(ext_is_mine, jnp.logical_or(dx_ext == 0, dx_ext == 1))
    goes_xd = jnp.logical_and(ext_is_mine, dx_ext == 0)

    def ext_forward():
        @pl.when(jnp.logical_not(own_diag))
        def _():
            to_zq.wait_recv()

        @pl.when(goes_xu)
        def _():
            to_xu.start()

        @pl.when(goes_xd)
        def _():
            to_xd.start()

        @pl.when(goes_zq)
        def _():
            to_zq.start()

    for c in range(CHILDREN):

        def find(block, at, c=c):
            hit = (anc[c, at] == block).astype(jnp.int32)
            slot_of[c, block] = at
            listed[c, block] = hit.astype(jnp.float32)
            return jnp.minimum(at + hit, MAX_ANC - 1)

        lax.fori_loop(0, ROOT_BLOCKS, find, jnp.int32(0))
    for at, (dx, zr) in enumerate(SOURCES):
        px, pz = (x + dx) % 4, zq if zr else z
        for t in range(2):
            unit_row[2 * at + t] = 2 * (px * 4 + pz) + t
            unit_win[2 * at + t] = window(px, pz, t)
    acc[...] = jnp.zeros_like(acc)
    part[...] = jnp.zeros_like(part)

    def build(c):
        for at, key in enumerate((3, 0, 2, 1, 3)):
            block = 4 * q + key
            slot, keep = slot_of[c, block], listed[c, block].astype(jnp.bfloat16)
            for zz in range(2):
                pk[c][at * BLK : (at + 1) * BLK, zz * 128 : (zz + 1) * 128] = (
                    pb[c][zz, slot // 6, slot % 6] * keep
                )

    def add(c, product, row):
        slot, keep = slot_of[c, row], listed[c, row]
        for zz in range(2):
            mine = pb[c][zz, slot // 6, slot % 6].astype(jnp.float32)
            term = product[:, zz * 128 : (zz + 1) * 128] * mine
            acc[c, zz] += jnp.sum(term.reshape(BLK // 8, 8, 128), axis=0) * keep

    def compute(c, lo, hi):
        def step(u, carry):
            start = pl.multiple_of(unit_win[u] * BLK, BLK)
            product = jnp.dot(
                rb[u], pk[c][pl.ds(start, 2 * BLK), :], preferred_element_type=jnp.float32
            )
            add(c, product, unit_row[u])
            return carry

        lax.fori_loop(lo, hi, step, 0)

    def compute_ext(c):
        start = pl.multiple_of(ext_key * BLK, BLK)
        product = jnp.dot(
            ext[...], pk[c][pl.ds(start, BLK), :], preferred_element_type=jnp.float32
        )
        add(c, product, ext_row)

    def after_b(c):
        b[c][0].wait_recv()
        b[c][1].wait_recv()
        du[c] = p_d_up(c)
        dd[c] = p_d_down(c)
        e[c] = [p_e(c, down), p_e(c, up)]

    def after_a(c):
        a[c].wait_recv()
        cc[c] = p_c(c)

    def after_c(c):
        cc[c][0].wait_recv()
        cc[c][1].wait_recv()
        do[c] = p_d_other(c)

    def after_d(c):
        du[c].wait_recv()
        if dd[c] is not None:
            dd[c].wait_recv()
        e[c].append(p_e(c, far))

    after_a(0)
    after_b(0)
    r_a0.wait_recv()
    r_c0 = send(unit(0, 1, 0), unit(3, 1, 0), d_xu), send(unit(0, 1, 0), unit(1, 1, 0), d_xd)
    r_b1[0].wait_recv()
    r_b1[1].wait_recv()
    half = BLK // 2
    r_d1 = (
        send(unit(3, 0, 1).at[pl.ds(0, half)], unit(2, 0, 1).at[pl.ds(0, half)], d_xu),
        send(unit(1, 0, 1).at[pl.ds(half, half)], unit(2, 0, 1).at[pl.ds(half, half)], d_xd),
    )
    r_e1 = [send(unit(3, 0, 1), unit(3, 1, 1), d_zq), send(unit(1, 0, 1), unit(1, 1, 1), d_zq)]
    ext_forward()
    after_c(0)
    a[2] = p_a(2)
    b[2] = p_b(2)
    after_a(1)
    after_b(1)
    after_d(0)
    r_b0[0].wait_recv()
    r_b0[1].wait_recv()
    r_d0u = send(unit(3, 0, 0), unit(2, 0, 0), d_xu)
    r_a1.wait_recv()
    r_d1[0].wait_recv()
    r_d1[1].wait_recv()
    r_e1.append(send(unit(2, 0, 1), unit(2, 1, 1), d_zq))
    after_c(1)
    r_c0[0].wait_recv()
    r_c0[1].wait_recv()
    r_d0d = send(unit(1, 1, 0), unit(2, 1, 0), d_xd)
    after_a(2)
    after_b(2)
    after_d(1)
    do[0].wait_recv()
    for copy in e[0]:
        copy.wait_recv()
    kids.append(p_core_all(0))
    late = [p_core(2, 0, y, 0, 3), p_core(2, 0, up, 0, 3), p_core(2, 0, down, 0, 3), p_core(2, 1, y, 0, 3)]
    after_c(2)
    kids[0].wait_recv()
    build(0)
    compute(0, 0, 8)
    after_d(2)
    late.append(p_core(2, 0, far, 0, 3))
    compute_ext(0)
    r_e1[0].wait_recv()
    r_e1[1].wait_recv()
    compute(0, 8, 12)
    do[1].wait_recv()
    for copy in e[1]:
        copy.wait_recv()
    kids.append(p_core_all(1))
    r_d0u.wait_recv()
    compute(0, 12, 14)
    kids[1].wait_recv()
    build(1)
    compute(1, 0, 14)
    compute_ext(1)
    r_d0d.wait_recv()
    r_e1[2].wait_recv()
    compute(0, 14, 16)
    compute(1, 14, 16)
    do[2].wait_recv()
    for copy in e[2]:
        copy.wait_recv()
    for py in (down, up, far):
        late.append(p_core(2, 1, py, 0, 3))
    for copy in late:
        copy.wait_recv()
    build(2)
    compute(2, 0, UNITS)
    compute_ext(2)

    for zz in range(2):
        for c in range(CHILDREN):
            part[zz, c : c + 1, :] = 2.0 * jnp.sum(acc[c, zz], axis=0, keepdims=True)
    mine = q * 2 + z % 2
    sums = []
    for n, g in enumerate(group):
        copy = pltpu.make_async_remote_copy(
            src_ref=part.at[g[2]],
            dst_ref=red.at[mine],
            send_sem=red_send.at[n],
            recv_sem=red_recv.at[n],
            device_id=member(*g),
            device_id_type=MESH,
        )
        copy.start()
        sums.append(copy)
    red[mine] = part[0]
    for copy in sent:
        copy.wait_send()

    @pl.when(goes_zq)
    def _():
        to_zq.wait_send()

    @pl.when(goes_xu)
    def _():
        to_xu.wait_send()

    @pl.when(goes_xd)
    def _():
        to_xd.wait_send()

    for copy in sums:
        copy.wait()
    total = red[0]
    for at in range(1, 16):
        total = total + red[at]
    out[...] = total


def per_device(ancestor_blocks, root_inverse, factor_rows, diag_inverse):
    vmem, smem, dma = pltpu.VMEM, pltpu.SMEM, pltpu.SemaphoreType.DMA
    rows = factor_rows.reshape(CHILDREN, 3, BLK, 128)
    total = pl.pallas_call(
        kernel,
        out_shape=jax.ShapeDtypeStruct((8, 128), jnp.float32),
        in_specs=[
            pl.BlockSpec(memory_space=smem),
            pl.BlockSpec(memory_space=pl.ANY),
            pl.BlockSpec(memory_space=pl.ANY),
        ],
        out_specs=pl.BlockSpec(memory_space=vmem),
        scratch_shapes=[vmem((2, 4, 6, BLK, 128), jnp.bfloat16)] * CHILDREN
        + [
            vmem((UNITS, BLK, 2 * BLK), jnp.bfloat16),
            vmem((BLK, BLK), jnp.bfloat16),
        ]
        + [vmem((5 * BLK, 2 * 128), jnp.bfloat16)] * CHILDREN
        + [
            vmem((CHILDREN, 2, 8, 128), jnp.float32),
            vmem((2, 8, 128), jnp.float32),
            vmem((16, 8, 128), jnp.float32),
            smem((CHILDREN, ROOT_BLOCKS), jnp.int32),
            smem((CHILDREN, ROOT_BLOCKS), jnp.float32),
            smem((UNITS,), jnp.int32),
            smem((UNITS,), jnp.int32),
            dma((8,)),
            dma((COPIES,)),
            dma((COPIES,)),
            dma((3,)),
            dma,
            dma((15,)),
            dma((15,)),
        ],
        compiler_params=pltpu.CompilerParams(
            collective_id=0, has_side_effects=True, vmem_limit_bytes=40 * 2**20
        ),
    )(ancestor_blocks, root_inverse, rows)
    return diag_inverse + total[:CHILDREN]


def solution(mesh):
    in_specs = (P(), P("prow", "pcol"), P(None, "pcol", "prow"), P(None, "prow"))
    out_specs = P(None, "prow")
    return jax.shard_map(
        per_device, mesh=mesh, in_specs=in_specs, out_specs=out_specs, check_vma=False
    )
```

```python
import jax
import jax.numpy as jnp
from jax import lax
from jax.experimental import pallas as pl
from jax.experimental.pallas import tpu as pltpu
from jax.sharding import PartitionSpec as P

MESH = pl.DeviceIdType.MESH
BLK = 256
CHILDREN = 3
ROOT_BLOCKS = 32
MAX_ANC = 24
Z_FIRST = (1, 2, 2)
FAR_UP = (1, 1, 0)
SOURCES = ((0, 0), (0, 1), (1, 0), (3, 0), (1, 1), (3, 1), (2, 0), (2, 1))
UNITS = 2 * len(SOURCES)
COPIES = 96


def pick(index, values):
    out = jnp.int32(values[0])
    for at, value in enumerate(values[1:], 1):
        out = jnp.where(index == at, jnp.int32(value), out)
    return out


def kernel(
    anc,
    root,
    rows,
    out,
    pb0,
    pb1,
    pb2,
    rb,
    ext,
    pk0,
    pk1,
    pk2,
    acc,
    part,
    red,
    slot_of,
    listed,
    unit_row,
    unit_win,
    local_sem,
    send_sem,
    recv_sem,
    ext_send,
    ext_recv,
    red_send,
    red_recv,
):
    pb, pk = (pb0, pb1, pb2), (pk0, pk1, pk2)
    p, q = lax.axis_index("prow"), lax.axis_index("pcol")
    x, z = p // 4, p % 4
    y, core = q // 2, q % 2
    zp = z + 1 - 2 * (z % 2)
    zq = (z + 3 + 2 * (z % 2)) % 4
    up, down, far = (y + 1) % 4, (y + 3) % 4, (y + 2) % 4

    def device(px, py, pz, pc):
        return (px * 4 + pz, py * 2 + pc)

    d_z = device(x, y, zp, core)
    d_yu, d_yd = device(x, up, z, core), device(x, down, z, core)
    d_zq = device(x, y, zq, core)
    d_xu, d_xd = device((x + 1) % 4, y, z, core), device((x + 3) % 4, y, z, core)
    d_core = device(x, y, z, 1 - core)

    def window(px, pz, t):
        diagonal = jnp.logical_and(px == y, pz // 2 == core)
        second = pz - 2 * core
        below = px * 4 + pz < 2 * q
        plain = 1 + 2 * jnp.where(below, t, 1 - t)
        special = jnp.where(second == 0, 1, 2) if t == 0 else jnp.where(second == 0, 3, 0)
        return jnp.where(diagonal, special, plain).astype(jnp.int32)

    own_diag = jnp.logical_and(x == y, z // 2 == core)
    z_ext = jnp.where(z // 2 == core, z, zq)
    ext_key = 1 + (z_ext - 2 * core)
    ext_row = 2 * (4 * y + z_ext) + 1

    local = []
    for c in range(CHILDREN):
        local.append(
            pltpu.make_async_copy(
                rows.at[c], pb[c].at[0, y, pl.ds(core * 3, 3)], local_sem.at[c]
            )
        )
    for t in range(2):
        win = window(x, z, t)
        for h, values in enumerate(((3, 0, 2, 1), (0, 2, 1, 3))):
            column = pl.multiple_of(pick(win, values) * BLK, BLK)
            local.append(
                pltpu.make_async_copy(
                    root.at[pl.ds(t * BLK, BLK), pl.ds(column, BLK)],
                    rb.at[t, :, pl.ds(h * BLK, BLK)],
                    local_sem.at[3 + 2 * t + h],
                )
            )
    ext_column = pl.multiple_of(jnp.where(z - 2 * core == 1, 2 * BLK, 0), BLK)
    local_ext = pltpu.make_async_copy(
        root.at[pl.ds(BLK, BLK), pl.ds(ext_column, BLK)], ext, local_sem.at[7]
    )
    for copy in local:
        copy.start()

    @pl.when(own_diag)
    def _():
        local_ext.start()

    group = [(dy, dc, dz) for dy in range(4) for dc in range(2) for dz in range(2)][1:]

    def member(dy, dc, dz):
        return device(x, (y + dy) % 4, zp if dz else z, 1 - core if dc else core)

    partners = [member(*g) for g in group] + [d_zq, d_xu, d_xd]
    barrier = pltpu.get_barrier_semaphore()
    for partner in partners:
        pl.semaphore_signal(barrier, inc=1, device_id=partner, device_id_type=MESH)
    for copy in local:
        copy.wait()

    @pl.when(own_diag)
    def _():
        local_ext.wait()
        for t in range(2):
            rb[t, :, 0:BLK] = rb[t, :, 0:BLK] * jnp.bfloat16(0.5)

    pl.semaphore_wait(barrier, len(partners))

    sent = []

    def send(src, dst, target):
        n = len(sent)
        copy = pltpu.make_async_remote_copy(
            src_ref=src,
            dst_ref=dst,
            send_sem=send_sem.at[n],
            recv_sem=recv_sem.at[n],
            device_id=target,
            device_id_type=MESH,
        )
        copy.start()
        sent.append(copy)
        return copy

    def slots(c, zz, py, lo, hi):
        return pb[c].at[zz, py, pl.ds(core * 3 + lo, hi - lo)]

    def unit(dx, zr, t):
        return rb.at[2 * SOURCES.index((dx, zr)) + t]

    def p_a(c):
        return send(slots(c, 0, y, 0, 3), slots(c, 1, y, 0, 3), d_z)

    def p_b(c):
        own = slots(c, 0, y, 0, 3)
        return send(own, own, d_yu), send(own, own, d_yd)

    def p_c(c):
        ref = slots(c, 1, y, 0, Z_FIRST[c])
        return send(ref, ref, d_yu), send(ref, ref, d_yd)

    def p_d_up(c):
        ref = slots(c, 0, down, 0, Z_FIRST[c] + FAR_UP[c])
        return send(ref, ref, d_yu)

    def p_d_down(c):
        if Z_FIRST[c] + FAR_UP[c] == 3:
            return None
        ref = slots(c, 0, up, Z_FIRST[c] + FAR_UP[c], 3)
        return send(ref, ref, d_yd)

    def p_d_other(c):
        ref = slots(c, 1, up, 0, Z_FIRST[c])
        return send(ref, ref, d_yd)

    def p_e(c, py):
        return send(slots(c, 0, py, Z_FIRST[c], 3), slots(c, 1, py, Z_FIRST[c], 3), d_z)

    def p_core(c, zz, py, lo, hi):
        ref = slots(c, zz, py, lo, hi)
        return send(ref, ref, d_core)

    def p_core_all(c):
        ref = pb[c].at[:, :, pl.ds(core * 3, 3)]
        return send(ref, ref, d_core)

    ext_is_mine = z_ext == z
    dx_ext = (x - y + 4) % 4

    def ext_copy(n, target):
        return pltpu.make_async_remote_copy(
            src_ref=ext,
            dst_ref=ext,
            send_sem=ext_send.at[n],
            recv_sem=ext_recv,
            device_id=target,
            device_id_type=MESH,
        )

    to_zq, to_xu, to_xd = ext_copy(0, d_zq), ext_copy(1, d_xu), ext_copy(2, d_xd)
    goes_zq = ext_is_mine
    goes_xu = jnp.logical_and(ext_is_mine, jnp.logical_or(dx_ext == 0, dx_ext == 1))
    goes_xd = jnp.logical_and(ext_is_mine, dx_ext == 0)

    near = jnp.logical_and(ext_is_mine, dx_ext % 2 == 1)
    opposite = jnp.logical_and(ext_is_mine, dx_ext == 2)

    def ext_on(here, more):
        @pl.when(here)
        def _():
            to_zq.wait_recv()

        if more:

            @pl.when(jnp.logical_and(here, dx_ext == 1))
            def _():
                to_xu.start()

        @pl.when(here)
        def _():
            to_zq.start()

    @pl.when(own_diag)
    def _():
        to_xu.start()
        to_xd.start()
        to_zq.start()

    a, b, cc, du, dd, do, e = {}, {}, {}, {}, {}, {}, {}
    kids = []
    a[0] = p_a(0)
    b[0] = p_b(0)
    r_a0 = send(unit(0, 0, 0), unit(0, 1, 0), d_zq)
    r_b1 = send(unit(0, 0, 1), unit(3, 0, 1), d_xu), send(unit(0, 0, 1), unit(1, 0, 1), d_xd)
    r_a1 = send(unit(0, 0, 1), unit(0, 1, 1), d_zq)
    r_b0 = send(unit(0, 0, 0), unit(3, 0, 0), d_xu), send(unit(0, 0, 0), unit(1, 0, 0), d_xd)
    a[1] = p_a(1)
    b[1] = p_b(1)

    for c in range(CHILDREN):

        def find(block, at, c=c):
            hit = (anc[c, at] == block).astype(jnp.int32)
            slot_of[c, block] = at
            listed[c, block] = hit.astype(jnp.float32)
            return jnp.minimum(at + hit, MAX_ANC - 1)

        lax.fori_loop(0, ROOT_BLOCKS, find, jnp.int32(0))
    for at, (dx, zr) in enumerate(SOURCES):
        px, pz = (x + dx) % 4, zq if zr else z
        for t in range(2):
            unit_row[2 * at + t] = 2 * (px * 4 + pz) + t
            unit_win[2 * at + t] = window(px, pz, t)
    acc[...] = jnp.zeros_like(acc)
    part[...] = jnp.zeros_like(part)

    def build(c):
        for at, key in enumerate((3, 0, 2, 1, 3)):
            block = 4 * q + key
            slot, keep = slot_of[c, block], listed[c, block].astype(jnp.bfloat16)
            for zz in range(2):
                pk[c][at * BLK : (at + 1) * BLK, zz * 128 : (zz + 1) * 128] = (
                    pb[c][zz, slot // 6, slot % 6] * keep
                )

    def add(c, product, row):
        slot, keep = slot_of[c, row], listed[c, row]
        for zz in range(2):
            mine = pb[c][zz, slot // 6, slot % 6].astype(jnp.float32)
            term = product[:, zz * 128 : (zz + 1) * 128] * mine
            acc[c, zz] += jnp.sum(term.reshape(BLK // 8, 8, 128), axis=0) * keep

    def compute(c, lo, hi):
        def step(u, carry):
            start = pl.multiple_of(unit_win[u] * BLK, BLK)
            product = jnp.dot(
                rb[u], pk[c][pl.ds(start, 2 * BLK), :], preferred_element_type=jnp.float32
            )
            add(c, product, unit_row[u])
            return carry

        lax.fori_loop(lo, hi, step, 0)

    def compute_ext(c):
        start = pl.multiple_of(ext_key * BLK, BLK)
        product = jnp.dot(
            ext[...], pk[c][pl.ds(start, BLK), :], preferred_element_type=jnp.float32
        )
        add(c, product, ext_row)

    def after_b(c):
        b[c][0].wait_recv()
        b[c][1].wait_recv()
        du[c] = p_d_up(c)
        dd[c] = p_d_down(c)
        e[c] = [p_e(c, down), p_e(c, up)]

    def after_a(c):
        a[c].wait_recv()
        cc[c] = p_c(c)

    def after_c(c):
        cc[c][0].wait_recv()
        cc[c][1].wait_recv()
        do[c] = p_d_other(c)

    def after_d(c):
        du[c].wait_recv()
        if dd[c] is not None:
            dd[c].wait_recv()
        e[c].append(p_e(c, far))

    after_a(0)
    after_b(0)
    r_a0.wait_recv()
    r_c0 = send(unit(0, 1, 0), unit(3, 1, 0), d_xu), send(unit(0, 1, 0), unit(1, 1, 0), d_xd)
    r_b1[0].wait_recv()
    r_b1[1].wait_recv()
    half = BLK // 2
    r_d1 = (
        send(unit(3, 0, 1).at[pl.ds(0, half)], unit(2, 0, 1).at[pl.ds(0, half)], d_xu),
        send(unit(1, 0, 1).at[pl.ds(half, half)], unit(2, 0, 1).at[pl.ds(half, half)], d_xd),
    )
    r_e1 = [send(unit(3, 0, 1), unit(3, 1, 1), d_zq), send(unit(1, 0, 1), unit(1, 1, 1), d_zq)]
    ext_on(near, True)
    after_c(0)
    a[2] = p_a(2)
    b[2] = p_b(2)
    after_a(1)
    after_b(1)
    after_d(0)
    r_b0[0].wait_recv()
    r_b0[1].wait_recv()
    r_d0u = send(unit(3, 0, 0), unit(2, 0, 0), d_xu)
    r_a1.wait_recv()
    r_d1[0].wait_recv()
    r_d1[1].wait_recv()
    r_e1.append(send(unit(2, 0, 1), unit(2, 1, 1), d_zq))
    after_c(1)
    r_c0[0].wait_recv()
    r_c0[1].wait_recv()
    r_d0d = send(unit(1, 1, 0), unit(2, 1, 0), d_xd)
    after_a(2)
    after_b(2)
    after_d(1)
    do[0].wait_recv()
    for copy in e[0]:
        copy.wait_recv()
    kids.append(p_core_all(0))
    ext_on(opposite, False)
    late = [p_core(2, 0, y, 0, 3), p_core(2, 0, up, 0, 3), p_core(2, 0, down, 0, 3), p_core(2, 1, y, 0, 3)]
    after_c(2)
    kids[0].wait_recv()
    build(0)
    compute(0, 0, 8)
    after_d(2)
    late.append(p_core(2, 0, far, 0, 3))
    r_e1[0].wait_recv()
    r_e1[1].wait_recv()
    compute(0, 8, 12)
    do[1].wait_recv()
    for copy in e[1]:
        copy.wait_recv()
    kids.append(p_core_all(1))
    r_d0u.wait_recv()
    compute(0, 12, 14)
    kids[1].wait_recv()
    build(1)
    compute(1, 0, 14)
    r_d0d.wait_recv()
    r_e1[2].wait_recv()
    compute(0, 14, 16)
    compute(1, 14, 16)
    do[2].wait_recv()
    for copy in e[2]:
        copy.wait_recv()
    for py in (down, up, far):
        late.append(p_core(2, 1, py, 0, 3))
    for copy in late:
        copy.wait_recv()
    build(2)
    compute(2, 0, UNITS)

    @pl.when(jnp.logical_not(ext_is_mine))
    def _():
        to_zq.wait_recv()

    for c in range(CHILDREN):
        compute_ext(c)

    for zz in range(2):
        for c in range(CHILDREN):
            part[zz, c : c + 1, :] = 2.0 * jnp.sum(acc[c, zz], axis=0, keepdims=True)
    mine = q * 2 + z % 2
    sums = []
    for n, g in enumerate(group):
        copy = pltpu.make_async_remote_copy(
            src_ref=part.at[g[2]],
            dst_ref=red.at[mine],
            send_sem=red_send.at[n],
            recv_sem=red_recv.at[n],
            device_id=member(*g),
            device_id_type=MESH,
        )
        copy.start()
        sums.append(copy)
    red[mine] = part[0]
    for copy in sent:
        copy.wait_send()

    @pl.when(goes_zq)
    def _():
        to_zq.wait_send()

    @pl.when(goes_xu)
    def _():
        to_xu.wait_send()

    @pl.when(goes_xd)
    def _():
        to_xd.wait_send()

    for copy in sums:
        copy.wait()
    total = red[0]
    for at in range(1, 16):
        total = total + red[at]
    out[...] = total


def per_device(ancestor_blocks, root_inverse, factor_rows, diag_inverse):
    vmem, smem, dma = pltpu.VMEM, pltpu.SMEM, pltpu.SemaphoreType.DMA
    rows = factor_rows.reshape(CHILDREN, 3, BLK, 128)
    total = pl.pallas_call(
        kernel,
        out_shape=jax.ShapeDtypeStruct((8, 128), jnp.float32),
        in_specs=[
            pl.BlockSpec(memory_space=smem),
            pl.BlockSpec(memory_space=pl.ANY),
            pl.BlockSpec(memory_space=pl.ANY),
        ],
        out_specs=pl.BlockSpec(memory_space=vmem),
        scratch_shapes=[vmem((2, 4, 6, BLK, 128), jnp.bfloat16)] * CHILDREN
        + [
            vmem((UNITS, BLK, 2 * BLK), jnp.bfloat16),
            vmem((BLK, BLK), jnp.bfloat16),
        ]
        + [vmem((5 * BLK, 2 * 128), jnp.bfloat16)] * CHILDREN
        + [
            vmem((CHILDREN, 2, 8, 128), jnp.float32),
            vmem((2, 8, 128), jnp.float32),
            vmem((16, 8, 128), jnp.float32),
            smem((CHILDREN, ROOT_BLOCKS), jnp.int32),
            smem((CHILDREN, ROOT_BLOCKS), jnp.float32),
            smem((UNITS,), jnp.int32),
            smem((UNITS,), jnp.int32),
            dma((8,)),
            dma((COPIES,)),
            dma((COPIES,)),
            dma((3,)),
            dma,
            dma((15,)),
            dma((15,)),
        ],
        compiler_params=pltpu.CompilerParams(
            collective_id=0, has_side_effects=True, vmem_limit_bytes=62 * 2**20
        ),
    )(ancestor_blocks, root_inverse, rows)
    return diag_inverse + total[:CHILDREN]


def solution(mesh):
    in_specs = (P(), P("prow", "pcol"), P(None, "pcol", "prow"), P(None, "prow"))
    out_specs = P(None, "prow")
    return jax.shard_map(
        per_device, mesh=mesh, in_specs=in_specs, out_specs=out_specs, check_vma=False
    )
```

```python
import jax
import jax.numpy as jnp
from jax import lax
from jax.experimental import pallas as pl
from jax.experimental.pallas import tpu as pltpu
from jax.sharding import PartitionSpec as P

MESH = pl.DeviceIdType.MESH
BLK = 256
CHILDREN = 3
ROOT_BLOCKS = 32
MAX_ANC = 24
Z_FIRST = (3, 0, 2)
FAR_UP = (0, 2, 0)
SOURCES = ((0, 0), (0, 1), (1, 0), (3, 0), (1, 1), (3, 1), (2, 0), (2, 1))
UNITS = 2 * len(SOURCES)
ORDER = (
    ("a0", "bd0", "bu0", "ra1", "rb0u", "rb1d", "a1", "bd1", "bu1", "ra0", "rb0d", "rb1u", "a2", "cd0", "cu0"),
    ("near", "rd0u", "rd1d", "re1u", "dd1", "du1", "ed1", "bd2", "bu2", "rc0d", "eu1", "rd1u", "re1d", "ks2"),
    ("do0", "du0", "rc0u", "ka1", "opposite", "ef1", "cd2", "rd0d", "re1f", "du2", "dd2", "ed2", "cu2", "eu2"),
    ("kb0", "ka0", "do2", "kb1", "ef2", "ka2", "ku2", "kd2", "kf2"),
)
COPIES = sum(len(line) for line in ORDER) - 2


def pick(index, values):
    out = jnp.int32(values[0])
    for at, value in enumerate(values[1:], 1):
        out = jnp.where(index == at, jnp.int32(value), out)
    return out


def kernel(
    anc,
    root,
    rows,
    out,
    pb0,
    pb1,
    pb2,
    rb,
    ext,
    pk0,
    pk1,
    pk2,
    part,
    red,
    slot_of,
    listed,
    local_sem,
    send_sem,
    recv_sem,
    ext_send,
    ext_recv,
    red_send,
    red_recv,
):
    pb, pk = (pb0, pb1, pb2), (pk0, pk1, pk2)
    p, q = lax.axis_index("prow"), lax.axis_index("pcol")
    x, z = p // 4, p % 4
    y, core = q // 2, q % 2
    zp = z + 1 - 2 * (z % 2)
    zq = (z + 3 + 2 * (z % 2)) % 4
    up, down, far = (y + 1) % 4, (y + 3) % 4, (y + 2) % 4

    def device(px, py, pz, pc):
        return (px * 4 + pz, py * 2 + pc)

    d_z = device(x, y, zp, core)
    d_yu, d_yd = device(x, up, z, core), device(x, down, z, core)
    d_zq = device(x, y, zq, core)
    d_xu, d_xd = device((x + 1) % 4, y, z, core), device((x + 3) % 4, y, z, core)
    d_core = device(x, y, z, 1 - core)

    def window(px, pz, t):
        diagonal = jnp.logical_and(px == y, pz // 2 == core)
        second = pz - 2 * core
        below = px * 4 + pz < 2 * q
        plain = 1 + 2 * jnp.where(below, t, 1 - t)
        special = jnp.where(second == 0, 1, 2) if t == 0 else jnp.where(second == 0, 3, 0)
        return jnp.where(diagonal, special, plain).astype(jnp.int32)

    own_diag = jnp.logical_and(x == y, z // 2 == core)
    z_ext = jnp.where(z // 2 == core, z, zq)
    ext_key = 1 + (z_ext - 2 * core)
    ext_row = 2 * (4 * y + z_ext) + 1

    local = []
    for c in range(CHILDREN):
        local.append(
            pltpu.make_async_copy(
                rows.at[c], pb[c].at[0, y, pl.ds(core * 3, 3)], local_sem.at[c]
            )
        )
    for t in range(2):
        win = window(x, z, t)
        for h, values in enumerate(((3, 0, 2, 1), (0, 2, 1, 3))):
            column = pl.multiple_of(pick(win, values) * BLK, BLK)
            local.append(
                pltpu.make_async_copy(
                    root.at[pl.ds(t * BLK, BLK), pl.ds(column, BLK)],
                    rb.at[t, :, pl.ds(h * BLK, BLK)],
                    local_sem.at[3 + 2 * t + h],
                )
            )
    ext_column = pl.multiple_of(jnp.where(z - 2 * core == 1, 2 * BLK, 0), BLK)
    local_ext = pltpu.make_async_copy(
        root.at[pl.ds(BLK, BLK), pl.ds(ext_column, BLK)], ext, local_sem.at[7]
    )
    for copy in local:
        copy.start()

    @pl.when(own_diag)
    def _():
        local_ext.start()

    group = [(dy, dc, dz) for dy in (2, 1, 3, 0) for dz in (1, 0) for dc in (1, 0)][:-1]

    def member(dy, dc, dz):
        return device(x, (y + dy) % 4, zp if dz else z, 1 - core if dc else core)

    partners = [d_z, d_yu, d_yd, d_core, d_zq, d_xu, d_xd]
    barrier = pltpu.get_barrier_semaphore()
    for partner in partners:
        pl.semaphore_signal(barrier, inc=1, device_id=partner, device_id_type=MESH)
    for copy in local:
        copy.wait()

    @pl.when(own_diag)
    def _():
        local_ext.wait()
        for t in range(2):
            rb[t, :, 0:BLK] = rb[t, :, 0:BLK] * jnp.bfloat16(0.5)

    pl.semaphore_wait(barrier, len(partners))

    sent, arrived = {}, set()

    def slots(c, zz, py, lo, hi):
        return pb[c].at[zz, py, pl.ds(core * 3 + lo, hi - lo)]

    def unit(dx, zr, t, lo=0, hi=BLK):
        ref = rb.at[2 * SOURCES.index((dx, zr)) + t]
        return ref if hi - lo == BLK else ref.at[pl.ds(lo, hi - lo)]

    def rows_copy(kind, c):
        m = Z_FIRST[c]
        split = m + FAR_UP[c]
        same = {
            "bu": (slots(c, 0, y, 0, 3), d_yu, ()),
            "bd": (slots(c, 0, y, 0, 3), d_yd, ()),
            "cu": (slots(c, 1, y, 0, m), d_yu, ("a",)),
            "cd": (slots(c, 1, y, 0, m), d_yd, ("a",)),
            "du": (slots(c, 0, down, 0, split), d_yu, ("bu",)),
            "dd": (slots(c, 0, up, split, 3), d_yd, ("bd",)),
            "do": (slots(c, 1, up, 0, m), d_yd, ("cd",)),
            "ka": (pb[c].at[0, :, pl.ds(core * 3, 3)], d_core, ("bu", "bd", "du", "dd")),
            "kb": (pb[c].at[1, :, pl.ds(core * 3, 3)], d_core, ("a", "cu", "cd", "do", "eu", "ed", "ef")),
            "ks": (slots(c, 1, y, 0, 3), d_core, ("a",)),
            "kd": (slots(c, 1, down, 0, 3), d_core, ("cu", "ed")),
            "ku": (slots(c, 1, up, 0, 3), d_core, ("cd", "eu")),
            "kf": (slots(c, 1, far, 0, 3), d_core, ("do", "ef")),
        }
        over = {
            "a": (y, 0, ()),
            "ed": (down, m, ("bu",)),
            "eu": (up, m, ("bd",)),
            "ef": (far, m, ("du", "dd")),
        }
        if kind in same:
            ref, target, first = same[kind]
            return ref, ref, target, first
        py, lo, first = over[kind]
        return slots(c, 0, py, lo, 3), slots(c, 1, py, lo, 3), d_z, first

    half = BLK // 2
    root_copies = {
        "ra0": (unit(0, 0, 0), unit(0, 1, 0), d_zq, ()),
        "ra1": (unit(0, 0, 1), unit(0, 1, 1), d_zq, ()),
        "rb0u": (unit(0, 0, 0), unit(3, 0, 0), d_xu, ()),
        "rb0d": (unit(0, 0, 0), unit(1, 0, 0), d_xd, ()),
        "rb1u": (unit(0, 0, 1), unit(3, 0, 1), d_xu, ()),
        "rb1d": (unit(0, 0, 1), unit(1, 0, 1), d_xd, ()),
        "rc0u": (unit(0, 1, 0), unit(3, 1, 0), d_xu, ("ra0",)),
        "rc0d": (unit(0, 1, 0), unit(1, 1, 0), d_xd, ("ra0",)),
        "rd0u": (unit(3, 0, 0), unit(2, 0, 0), d_xu, ("rb0u",)),
        "rd0d": (unit(1, 1, 0), unit(2, 1, 0), d_xd, ("rc0d",)),
        "rd1u": (unit(3, 0, 1, 0, half), unit(2, 0, 1, 0, half), d_xu, ("rb1u",)),
        "rd1d": (unit(1, 0, 1, half, BLK), unit(2, 0, 1, half, BLK), d_xd, ("rb1d",)),
        "re1d": (unit(3, 0, 1), unit(3, 1, 1), d_zq, ("rb1u",)),
        "re1u": (unit(1, 0, 1), unit(1, 1, 1), d_zq, ("rb1d",)),
        "re1f": (unit(2, 0, 1), unit(2, 1, 1), d_zq, ("rd1u", "rd1d")),
    }

    def arrive(names):
        for name in names:
            if name in sent and name not in arrived:
                sent[name].wait_recv()
                arrived.add(name)

    def send(name):
        if name in root_copies:
            src, dst, target, first = root_copies[name]
        else:
            src, dst, target, first = rows_copy(name[:-1], int(name[-1]))
            first = [kind + name[-1] for kind in first]
        arrive(first)
        n = len(sent)
        sent[name] = pltpu.make_async_remote_copy(
            src_ref=src,
            dst_ref=dst,
            send_sem=send_sem.at[n],
            recv_sem=recv_sem.at[n],
            device_id=target,
            device_id_type=MESH,
        )
        sent[name].start()

    ext_is_mine = z_ext == z
    dx_ext = (x - y + 4) % 4

    def ext_copy(n, target):
        return pltpu.make_async_remote_copy(
            src_ref=ext,
            dst_ref=ext,
            send_sem=ext_send.at[n],
            recv_sem=ext_recv,
            device_id=target,
            device_id_type=MESH,
        )

    to_zq, to_xu, to_xd = ext_copy(0, d_zq), ext_copy(1, d_xu), ext_copy(2, d_xd)
    goes_zq = ext_is_mine
    goes_xu = jnp.logical_and(ext_is_mine, jnp.logical_or(dx_ext == 0, dx_ext == 1))
    goes_xd = jnp.logical_and(ext_is_mine, dx_ext == 0)

    near = jnp.logical_and(ext_is_mine, dx_ext % 2 == 1)
    opposite = jnp.logical_and(ext_is_mine, dx_ext == 2)

    def ext_on(here, more):
        @pl.when(here)
        def _():
            to_zq.wait_recv()

        if more:

            @pl.when(jnp.logical_and(here, dx_ext == 1))
            def _():
                to_xu.start()

        @pl.when(here)
        def _():
            to_zq.start()

    @pl.when(own_diag)
    def _():
        to_xu.start()
        to_xd.start()
        to_zq.start()

    for name in ORDER[0]:
        send(name)

    for c in range(CHILDREN):

        def find(block, at, c=c):
            hit = (anc[c, at] == block).astype(jnp.int32)
            slot_of[c, block] = at
            listed[c, block] = hit.astype(jnp.float32)
            return jnp.minimum(at + hit, MAX_ANC - 1)

        lax.fori_loop(0, ROOT_BLOCKS, find, jnp.int32(0))
    part[...] = jnp.zeros_like(part)
    units = []
    for dx, zr in SOURCES:
        px, pz = (x + dx) % 4, zq if zr else z
        units += [(2 * (px * 4 + pz) + t, window(px, pz, t)) for t in range(2)]

    def build(c):
        for at, key in enumerate((3, 0, 2, 1, 3)):
            block = 4 * q + key
            slot, keep = slot_of[c, block], listed[c, block].astype(jnp.bfloat16)
            for zz in range(2):
                pk[c][at * BLK : (at + 1) * BLK, zz * 128 : (zz + 1) * 128] = (
                    pb[c][zz, slot // 6, slot % 6] * keep
                )

    acc = [[jnp.zeros((8, 128), jnp.float32)] * 2 for _ in range(CHILDREN)]

    def add(c, product, row):
        slot, keep = slot_of[c, row], listed[c, row]
        for zz in range(2):
            mine = pb[c][zz, slot // 6, slot % 6].astype(jnp.float32)
            term = product[:, zz * 128 : (zz + 1) * 128] * mine
            acc[c][zz] = acc[c][zz] + jnp.sum(term.reshape(BLK // 8, 8, 128), axis=0) * keep

    def compute(c):
        for u, (row, win) in enumerate(units):
            start = pl.multiple_of(win * BLK, BLK)
            product = jnp.dot(
                rb[u], pk[c][pl.ds(start, 2 * BLK), :], preferred_element_type=jnp.float32
            )
            add(c, product, row)
        start = pl.multiple_of(ext_key * BLK, BLK)
        product = jnp.dot(
            ext[...], pk[c][pl.ds(start, BLK), :], preferred_element_type=jnp.float32
        )
        add(c, product, ext_row)

    for name in ORDER[1] + ORDER[2] + ORDER[3]:
        if name == "near":
            ext_on(near, True)
        elif name == "opposite":
            ext_on(opposite, False)
        else:
            send(name)

    arrive(root_copies)

    @pl.when(jnp.logical_not(ext_is_mine))
    def _():
        to_zq.wait_recv()

    for c in range(CHILDREN):
        arrive([name for name in sent if name not in root_copies and name[-1] == str(c)])
        build(c)
        compute(c)

    for zz in range(2):
        for c in range(CHILDREN):
            part[zz, c : c + 1, :] = 2.0 * jnp.sum(acc[c][zz], axis=0, keepdims=True)
    mine = q * 2 + z % 2
    sums = []
    for n, g in enumerate(group):
        copy = pltpu.make_async_remote_copy(
            src_ref=part.at[g[2]],
            dst_ref=red.at[mine],
            send_sem=red_send.at[n],
            recv_sem=red_recv.at[n],
            device_id=member(*g),
            device_id_type=MESH,
        )
        copy.start()
        sums.append(copy)
    red[mine] = part[0]
    for copy in sent.values():
        copy.wait_send()

    @pl.when(goes_zq)
    def _():
        to_zq.wait_send()

    @pl.when(goes_xu)
    def _():
        to_xu.wait_send()

    @pl.when(goes_xd)
    def _():
        to_xd.wait_send()

    for copy in sums:
        copy.wait()
    total = red[0]
    for at in range(1, 16):
        total = total + red[at]
    out[...] = total


def per_device(ancestor_blocks, root_inverse, factor_rows, diag_inverse):
    vmem, smem, dma = pltpu.VMEM, pltpu.SMEM, pltpu.SemaphoreType.DMA
    rows = factor_rows.reshape(CHILDREN, 3, BLK, 128)
    total = pl.pallas_call(
        kernel,
        out_shape=jax.ShapeDtypeStruct((8, 128), jnp.float32),
        in_specs=[
            pl.BlockSpec(memory_space=smem),
            pl.BlockSpec(memory_space=pl.ANY),
            pl.BlockSpec(memory_space=pl.ANY),
        ],
        out_specs=pl.BlockSpec(memory_space=vmem),
        scratch_shapes=[vmem((2, 4, 6, BLK, 128), jnp.bfloat16)] * CHILDREN
        + [
            vmem((UNITS, BLK, 2 * BLK), jnp.bfloat16),
            vmem((BLK, BLK), jnp.bfloat16),
        ]
        + [vmem((5 * BLK, 2 * 128), jnp.bfloat16)] * CHILDREN
        + [
            vmem((2, 8, 128), jnp.float32),
            vmem((16, 8, 128), jnp.float32),
            smem((CHILDREN, ROOT_BLOCKS), jnp.int32),
            smem((CHILDREN, ROOT_BLOCKS), jnp.float32),
            dma((8,)),
            dma((COPIES,)),
            dma((COPIES,)),
            dma((3,)),
            dma,
            dma((15,)),
            dma((15,)),
        ],
        compiler_params=pltpu.CompilerParams(
            collective_id=0, has_side_effects=True, vmem_limit_bytes=62 * 2**20
        ),
    )(ancestor_blocks, root_inverse, rows)
    return diag_inverse + total[:CHILDREN]


def solution(mesh):
    in_specs = (P(), P("prow", "pcol"), P(None, "pcol", "prow"), P(None, "prow"))
    out_specs = P(None, "prow")
    return jax.shard_map(
        per_device, mesh=mesh, in_specs=in_specs, out_specs=out_specs, check_vma=False
    )
```

```python
import jax
import jax.numpy as jnp
from jax import lax
from jax.experimental import pallas as pl
from jax.experimental.pallas import tpu as pltpu
from jax.sharding import PartitionSpec as P

MESH = pl.DeviceIdType.MESH
BLK = 256
CHILDREN = 3
ROOT_BLOCKS = 32
MAX_ANC = 24
Z_FIRST = (3, 0, 2)
FAR_UP = (0, 2, 0)
SOURCES = ((0, 0), (0, 1), (1, 0), (3, 0), (1, 1), (3, 1), (2, 0), (2, 1))
UNITS = 2 * len(SOURCES)
ORDER = (
    ("a0", "bd0", "bu0", "ra1", "rb0u", "rb1d", "a1", "bd1", "bu1", "ra0", "rb0d", "rb1u", "a2", "cd0"),
    ("cu0", "near", "rd0u", "rd1d", "re1u", "dd1", "du1", "ed1", "bd2", "bu2", "rc0d", "eu1", "rd1u", "re1d"),
    ("ks2", "do0", "du0", "rc0u", "ka1", "opposite", "ef1", "cd2", "rd0d", "re1f", "du2", "dd2", "ed2", "cu2"),
    ("eu2", "kb0", "ka0", "do2", "kb1", "ef2", "ka2", "sum0", "sum1", "ku2", "kd2", "kf2"),
)
ORDER = sum(ORDER, ())
OTHER = ("near", "opposite", "sum0", "sum1")
COPIES = len(ORDER) - len(OTHER)


def pick(index, values):
    out = jnp.int32(values[0])
    for at, value in enumerate(values[1:], 1):
        out = jnp.where(index == at, jnp.int32(value), out)
    return out


def kernel(
    anc_hbm,
    root,
    rows,
    out,
    pb0,
    pb1,
    pb2,
    rb,
    ext,
    pk0,
    pk1,
    pk2,
    part,
    red,
    anc,
    slot_of,
    listed,
    local_sem,
    send_sem,
    recv_sem,
    ext_send,
    ext_recv,
    red_send,
    red_recv,
):
    pb, pk = (pb0, pb1, pb2), (pk0, pk1, pk2)
    p, q = lax.axis_index("prow"), lax.axis_index("pcol")
    x, z = p // 4, p % 4
    y, core = q // 2, q % 2
    zp = z + 1 - 2 * (z % 2)
    zq = (z + 3 + 2 * (z % 2)) % 4
    up, down, far = (y + 1) % 4, (y + 3) % 4, (y + 2) % 4

    def device(px, py, pz, pc):
        return (px * 4 + pz, py * 2 + pc)

    d_z = device(x, y, zp, core)
    d_yu, d_yd = device(x, up, z, core), device(x, down, z, core)
    d_zq = device(x, y, zq, core)
    d_xu, d_xd = device((x + 1) % 4, y, z, core), device((x + 3) % 4, y, z, core)
    d_core = device(x, y, z, 1 - core)

    group = [(dy, dc, dz) for dy in (2, 1, 3, 0) for dz in (1, 0) for dc in (1, 0)][:-1]

    def member(dy, dc, dz):
        return device(x, (y + dy) % 4, zp if dz else z, 1 - core if dc else core)

    partners = [d_z, d_yu, d_yd, d_core, d_zq, d_xu, d_xd]
    barrier = pltpu.get_barrier_semaphore()
    for partner in partners:
        pl.semaphore_signal(barrier, inc=1, device_id=partner, device_id_type=MESH)
    def window(px, pz, t):
        diagonal = jnp.logical_and(px == y, pz // 2 == core)
        second = pz - 2 * core
        below = px * 4 + pz < 2 * q
        plain = 1 + 2 * jnp.where(below, t, 1 - t)
        special = jnp.where(second == 0, 1, 2) if t == 0 else jnp.where(second == 0, 3, 0)
        return jnp.where(diagonal, special, plain).astype(jnp.int32)

    own_diag = jnp.logical_and(x == y, z // 2 == core)
    z_ext = jnp.where(z // 2 == core, z, zq)
    ext_key = 1 + (z_ext - 2 * core)
    ext_row = 2 * (4 * y + z_ext) + 1

    local = []
    for c in range(CHILDREN):
        local.append(
            pltpu.make_async_copy(
                rows.at[c], pb[c].at[0, y, pl.ds(core * 3, 3)], local_sem.at[c]
            )
        )
    for t in range(2):
        win = window(x, z, t)
        for h, values in enumerate(((3, 0, 2, 1), (0, 2, 1, 3))):
            column = pl.multiple_of(pick(win, values) * BLK, BLK)
            local.append(
                pltpu.make_async_copy(
                    root.at[pl.ds(t * BLK, BLK), pl.ds(column, BLK)],
                    rb.at[t, :, pl.ds(h * BLK, BLK)],
                    local_sem.at[3 + 2 * t + h],
                )
            )
    ext_column = pl.multiple_of(jnp.where(z - 2 * core == 1, 2 * BLK, 0), BLK)
    local_ext = pltpu.make_async_copy(
        root.at[pl.ds(BLK, BLK), pl.ds(ext_column, BLK)], ext, local_sem.at[7]
    )
    for copy in local:
        copy.start()
    blocks = pltpu.make_async_copy(anc_hbm, anc, local_sem.at[8])
    blocks.start()

    @pl.when(own_diag)
    def _():
        local_ext.start()

    for copy in local:
        copy.wait()

    @pl.when(own_diag)
    def _():
        local_ext.wait()
        for t in range(2):
            rb[t, :, 0:BLK] = rb[t, :, 0:BLK] * jnp.bfloat16(0.5)

    pl.semaphore_wait(barrier, len(partners))

    sent, arrived = {}, set()

    def slots(c, zz, py, lo, hi):
        return pb[c].at[zz, py, pl.ds(core * 3 + lo, hi - lo)]

    def unit(dx, zr, t, lo=0, hi=BLK):
        ref = rb.at[2 * SOURCES.index((dx, zr)) + t]
        return ref if hi - lo == BLK else ref.at[pl.ds(lo, hi - lo)]

    def rows_copy(kind, c):
        m = Z_FIRST[c]
        split = m + FAR_UP[c]
        same = {
            "bu": (slots(c, 0, y, 0, 3), d_yu, ()),
            "bd": (slots(c, 0, y, 0, 3), d_yd, ()),
            "cu": (slots(c, 1, y, 0, m), d_yu, ("a",)),
            "cd": (slots(c, 1, y, 0, m), d_yd, ("a",)),
            "du": (slots(c, 0, down, 0, split), d_yu, ("bu",)),
            "dd": (slots(c, 0, up, split, 3), d_yd, ("bd",)),
            "do": (slots(c, 1, up, 0, m), d_yd, ("cd",)),
            "ka": (pb[c].at[0, :, pl.ds(core * 3, 3)], d_core, ("bu", "bd", "du", "dd")),
            "kb": (pb[c].at[1, :, pl.ds(core * 3, 3)], d_core, ("a", "cu", "cd", "do", "eu", "ed", "ef")),
            "ks": (slots(c, 1, y, 0, 3), d_core, ("a",)),
            "kd": (slots(c, 1, down, 0, 3), d_core, ("cu", "ed")),
            "ku": (slots(c, 1, up, 0, 3), d_core, ("cd", "eu")),
            "kf": (slots(c, 1, far, 0, 3), d_core, ("do", "ef")),
        }
        over = {
            "a": (y, 0, ()),
            "ed": (down, m, ("bu",)),
            "eu": (up, m, ("bd",)),
            "ef": (far, m, ("du", "dd")),
        }
        if kind in same:
            ref, target, first = same[kind]
            return ref, ref, target, first
        py, lo, first = over[kind]
        return slots(c, 0, py, lo, 3), slots(c, 1, py, lo, 3), d_z, first

    half = BLK // 2
    root_copies = {
        "ra0": (unit(0, 0, 0), unit(0, 1, 0), d_zq, ()),
        "ra1": (unit(0, 0, 1), unit(0, 1, 1), d_zq, ()),
        "rb0u": (unit(0, 0, 0), unit(3, 0, 0), d_xu, ()),
        "rb0d": (unit(0, 0, 0), unit(1, 0, 0), d_xd, ()),
        "rb1u": (unit(0, 0, 1), unit(3, 0, 1), d_xu, ()),
        "rb1d": (unit(0, 0, 1), unit(1, 0, 1), d_xd, ()),
        "rc0u": (unit(0, 1, 0), unit(3, 1, 0), d_xu, ("ra0",)),
        "rc0d": (unit(0, 1, 0), unit(1, 1, 0), d_xd, ("ra0",)),
        "rd0u": (unit(3, 0, 0), unit(2, 0, 0), d_xu, ("rb0u",)),
        "rd0d": (unit(1, 1, 0), unit(2, 1, 0), d_xd, ("rc0d",)),
        "rd1u": (unit(3, 0, 1, 0, half), unit(2, 0, 1, 0, half), d_xu, ("rb1u",)),
        "rd1d": (unit(1, 0, 1, half, BLK), unit(2, 0, 1, half, BLK), d_xd, ("rb1d",)),
        "re1d": (unit(3, 0, 1), unit(3, 1, 1), d_zq, ("rb1u",)),
        "re1u": (unit(1, 0, 1), unit(1, 1, 1), d_zq, ("rb1d",)),
        "re1f": (unit(2, 0, 1), unit(2, 1, 1), d_zq, ("rd1u", "rd1d")),
    }

    def arrive(names):
        for name in names:
            if name in sent and name not in arrived:
                sent[name].wait_recv()
                arrived.add(name)

    def send(name):
        if name in root_copies:
            src, dst, target, first = root_copies[name]
        else:
            src, dst, target, first = rows_copy(name[:-1], int(name[-1]))
            first = [kind + name[-1] for kind in first]
        arrive(first)
        n = len(sent)
        sent[name] = pltpu.make_async_remote_copy(
            src_ref=src,
            dst_ref=dst,
            send_sem=send_sem.at[n],
            recv_sem=recv_sem.at[n],
            device_id=target,
            device_id_type=MESH,
        )
        sent[name].start()

    ext_is_mine = z_ext == z
    dx_ext = (x - y + 4) % 4

    def ext_copy(n, target):
        return pltpu.make_async_remote_copy(
            src_ref=ext,
            dst_ref=ext,
            send_sem=ext_send.at[n],
            recv_sem=ext_recv,
            device_id=target,
            device_id_type=MESH,
        )

    to_zq, to_xu, to_xd = ext_copy(0, d_zq), ext_copy(1, d_xu), ext_copy(2, d_xd)
    goes_zq = ext_is_mine
    goes_xu = jnp.logical_and(ext_is_mine, jnp.logical_or(dx_ext == 0, dx_ext == 1))
    goes_xd = jnp.logical_and(ext_is_mine, dx_ext == 0)

    near = jnp.logical_and(ext_is_mine, dx_ext % 2 == 1)
    opposite = jnp.logical_and(ext_is_mine, dx_ext == 2)

    def ext_on(here, more):
        @pl.when(here)
        def _():
            to_zq.wait_recv()

        if more:

            @pl.when(jnp.logical_and(here, dx_ext == 1))
            def _():
                to_xu.start()

        @pl.when(here)
        def _():
            to_zq.start()

    @pl.when(own_diag)
    def _():
        to_xu.start()
        to_xd.start()
        to_zq.start()

    free = next(n for n, name in enumerate(ORDER) if name[0] in "cdek")
    for name in ORDER[:free]:
        send(name)

    blocks.wait()
    for c in range(CHILDREN):

        def find(block, at, c=c):
            hit = (anc[c, at] == block).astype(jnp.int32)
            slot_of[c, block] = at
            listed[c, block] = hit.astype(jnp.float32)
            return jnp.minimum(at + hit, MAX_ANC - 1)

        lax.fori_loop(0, ROOT_BLOCKS, find, jnp.int32(0))
    part[...] = jnp.zeros_like(part)
    units = []
    for dx, zr in SOURCES:
        px, pz = (x + dx) % 4, zq if zr else z
        units += [(2 * (px * 4 + pz) + t, window(px, pz, t)) for t in range(2)]

    def build(c):
        for at, key in enumerate((3, 0, 2, 1, 3)):
            block = 4 * q + key
            slot, keep = slot_of[c, block], listed[c, block].astype(jnp.bfloat16)
            for zz in range(2):
                pk[c][at * BLK : (at + 1) * BLK, zz * 128 : (zz + 1) * 128] = (
                    pb[c][zz, slot // 6, slot % 6] * keep
                )

    acc = [[jnp.zeros((8, 128), jnp.float32)] * 2 for _ in range(CHILDREN)]

    def add(c, product, row):
        slot, keep = slot_of[c, row], listed[c, row]
        for zz in range(2):
            mine = pb[c][zz, slot // 6, slot % 6].astype(jnp.float32)
            term = product[:, zz * 128 : (zz + 1) * 128] * mine
            acc[c][zz] = acc[c][zz] + jnp.sum(term.reshape(BLK // 8, 8, 128), axis=0) * keep

    brought = (
        ((), ()),
        (("ra0",), ("ra1",)),
        (("rb0d",), ("rb1d",)),
        (("rb0u",), ("rb1u",)),
        (("rc0d",), ("re1u",)),
        (("rc0u",), ("re1d",)),
        (("rd0u",), ("rd1u", "rd1d")),
        (("rd0d",), ("re1f",)),
    )
    late = UNITS - 2

    def compute(c, lo, hi):
        for u in range(lo, hi):
            arrive(brought[u // 2][u % 2])
            row, win = units[u]
            start = pl.multiple_of(win * BLK, BLK)
            product = jnp.dot(
                rb[u], pk[c][pl.ds(start, 2 * BLK), :], preferred_element_type=jnp.float32
            )
            add(c, product, row)

    def compute_ext(c):
        start = pl.multiple_of(ext_key * BLK, BLK)
        product = jnp.dot(
            ext[...], pk[c][pl.ds(start, BLK), :], preferred_element_type=jnp.float32
        )
        add(c, product, ext_row)

    def complete(c):
        arrive([name for name in sent if name[0] != "r" and name[-1] == str(c)])
        build(c)

    for name in ORDER[free:]:
        if name == "near":
            ext_on(near, True)
        elif name == "opposite":
            ext_on(opposite, False)
        elif name[:3] == "sum":
            complete(int(name[3]))
            compute(int(name[3]), 0, late)
        else:
            send(name)

    @pl.when(jnp.logical_not(ext_is_mine))
    def _():
        to_zq.wait_recv()

    for c in range(2):
        compute(c, late, UNITS)
        compute_ext(c)
    gone = [name for name in sent if name[0] != "k"]
    for name in gone:
        sent[name].wait_send()

    @pl.when(goes_zq)
    def _():
        to_zq.wait_send()

    @pl.when(goes_xu)
    def _():
        to_xu.wait_send()

    @pl.when(goes_xd)
    def _():
        to_xd.wait_send()

    complete(2)
    compute(2, 0, UNITS)
    compute_ext(2)

    for zz in range(2):
        for c in range(CHILDREN):
            part[zz, c : c + 1, :] = 2.0 * jnp.sum(acc[c][zz], axis=0, keepdims=True)
    mine = q * 2 + z % 2
    for g in group:
        pltpu.make_async_remote_copy(
            src_ref=part.at[g[2]],
            dst_ref=red.at[mine],
            send_sem=red_send,
            recv_sem=red_recv,
            device_id=member(*g),
            device_id_type=MESH,
        ).start()
    red[mine] = part[0]
    for name in sent:
        if name not in gone:
            sent[name].wait_send()
    every = pltpu.make_async_remote_copy(
        src_ref=red.at[pl.ds(0, 15)],
        dst_ref=red.at[pl.ds(0, 15)],
        send_sem=red_send,
        recv_sem=red_recv,
        device_id=d_core,
        device_id_type=MESH,
    )
    every.wait_recv()
    every.wait_send()
    total = red[0]
    for at in range(1, 16):
        total = total + red[at]
    out[...] = total


def per_device(ancestor_blocks, root_inverse, factor_rows, diag_inverse):
    vmem, smem, dma = pltpu.VMEM, pltpu.SMEM, pltpu.SemaphoreType.DMA
    rows = factor_rows.reshape(CHILDREN, 3, BLK, 128)
    total = pl.pallas_call(
        kernel,
        out_shape=vmem((8, 128), jnp.float32),
        in_specs=[
            pl.BlockSpec(memory_space=pl.ANY),
            pl.BlockSpec(memory_space=pl.ANY),
            pl.BlockSpec(memory_space=pl.ANY),
        ],
        out_specs=pl.BlockSpec(memory_space=vmem),
        scratch_shapes=[vmem((2, 4, 6, BLK, 128), jnp.bfloat16)] * CHILDREN
        + [
            vmem((UNITS, BLK, 2 * BLK), jnp.bfloat16),
            vmem((BLK, BLK), jnp.bfloat16),
        ]
        + [vmem((5 * BLK, 2 * 128), jnp.bfloat16)] * CHILDREN
        + [
            vmem((2, 8, 128), jnp.float32),
            vmem((16, 8, 128), jnp.float32),
            smem((CHILDREN, MAX_ANC), jnp.int32),
            smem((CHILDREN, ROOT_BLOCKS), jnp.int32),
            smem((CHILDREN, ROOT_BLOCKS), jnp.float32),
            dma((9,)),
            dma((COPIES,)),
            dma((COPIES,)),
            dma((3,)),
            dma,
            dma,
            dma,
        ],
        compiler_params=pltpu.CompilerParams(
            collective_id=0, has_side_effects=True, vmem_limit_bytes=62 * 2**20
        ),
    )(ancestor_blocks, root_inverse, rows)
    return diag_inverse + total[:CHILDREN]


def solution(mesh):
    in_specs = (P(), P("prow", "pcol"), P(None, "pcol", "prow"), P(None, "prow"))
    out_specs = P(None, "prow")
    return jax.shard_map(
        per_device, mesh=mesh, in_specs=in_specs, out_specs=out_specs, check_vma=False
    )
```

```python
import jax
import jax.numpy as jnp
from jax import lax
from jax.experimental import pallas as pl
from jax.experimental.pallas import tpu as pltpu
from jax.sharding import PartitionSpec as P

MESH = pl.DeviceIdType.MESH
BLK = 256
CHILDREN = 3
ROOT_BLOCKS = 32
MAX_ANC = 24
Z_FIRST = (3, 0, 2)
FAR_UP = (0, 2, 0)
SOURCES = ((0, 0), (0, 1), (1, 0), (3, 0), (1, 1), (3, 1), (2, 0), (2, 1))
UNITS = 2 * len(SOURCES)
ORDER = (
    ("bd0", "bu1", "rb1d", "a0", "bd1", "ra0", "rb1u", "a1", "bu0", "bu2", "ra1", "cd0", "ed1"),
    ("rb0u", "a2", "rb0d", "rc0d", "rd1d", "re1u", "du1", "re1d", "near", "dd1", "bd2", "rd1u", "do0"),
    ("du0", "rc0u", "eu1", "cu0", "du2", "ef1", "cd2", "opposite", "rd0d", "rd0u", "eu2", "ka0", "ka1"),
    ("ed2", "re1f", "cu2", "dd2", "kb0", "do2", "kb1", "ef2", "m0:0:8", "ka2", "m1:12:14", "ku2", "m0:12:14"),
    ("m1:8:12", "kd2", "ks2", "m0:14:16", "kf2", "m0:8:12", "m1:0:8", "m1:14:16", "m2:8:14", "m2:0:8", "m2:14:16"),
)
ORDER = sum(ORDER, ())
COPIES = sum(name[0] in "abcdekr" for name in ORDER)


def pick(index, values):
    out = jnp.int32(values[0])
    for at, value in enumerate(values[1:], 1):
        out = jnp.where(index == at, jnp.int32(value), out)
    return out


def kernel(
    anc_hbm,
    root,
    rows,
    out,
    pb0,
    pb1,
    pb2,
    rb,
    ext,
    pk0,
    pk1,
    pk2,
    part,
    red,
    anc,
    slot_of,
    listed,
    local_sem,
    send_sem,
    recv_sem,
    ext_send,
    ext_recv,
    red_send,
    red_recv,
):
    pb, pk = (pb0, pb1, pb2), (pk0, pk1, pk2)
    p, q = lax.axis_index("prow"), lax.axis_index("pcol")
    x, z = p // 4, p % 4
    y, core = q // 2, q % 2
    zp = z + 1 - 2 * (z % 2)
    zq = (z + 3 + 2 * (z % 2)) % 4
    up, down, far = (y + 1) % 4, (y + 3) % 4, (y + 2) % 4

    def device(px, py, pz, pc):
        return (px * 4 + pz, py * 2 + pc)

    d_z = device(x, y, zp, core)
    d_yu, d_yd = device(x, up, z, core), device(x, down, z, core)
    d_zq = device(x, y, zq, core)
    d_xu, d_xd = device((x + 1) % 4, y, z, core), device((x + 3) % 4, y, z, core)
    d_core = device(x, y, z, 1 - core)

    group = [(dy, dc, dz) for dy in (2, 1, 3, 0) for dz in (1, 0) for dc in (1, 0)][:-1]

    def member(dy, dc, dz):
        return device(x, (y + dy) % 4, zp if dz else z, 1 - core if dc else core)

    partners = [d_z, d_yu, d_yd, d_core, d_zq, d_xu, d_xd]
    barrier = pltpu.get_barrier_semaphore()
    for partner in partners:
        pl.semaphore_signal(barrier, inc=1, device_id=partner, device_id_type=MESH)
    def window(px, pz, t):
        diagonal = jnp.logical_and(px == y, pz // 2 == core)
        second = pz - 2 * core
        below = px * 4 + pz < 2 * q
        plain = 1 + 2 * jnp.where(below, t, 1 - t)
        special = jnp.where(second == 0, 1, 2) if t == 0 else jnp.where(second == 0, 3, 0)
        return jnp.where(diagonal, special, plain).astype(jnp.int32)

    own_diag = jnp.logical_and(x == y, z // 2 == core)
    z_ext = jnp.where(z // 2 == core, z, zq)
    ext_key = 1 + (z_ext - 2 * core)
    ext_row = 2 * (4 * y + z_ext) + 1

    local = []
    for c in range(CHILDREN):
        local.append(
            pltpu.make_async_copy(
                rows.at[c], pb[c].at[0, y, pl.ds(core * 3, 3)], local_sem.at[c]
            )
        )
    for t in range(2):
        win = window(x, z, t)
        for h, values in enumerate(((3, 0, 2, 1), (0, 2, 1, 3))):
            column = pl.multiple_of(pick(win, values) * BLK, BLK)
            local.append(
                pltpu.make_async_copy(
                    root.at[pl.ds(t * BLK, BLK), pl.ds(column, BLK)],
                    rb.at[t, :, pl.ds(h * BLK, BLK)],
                    local_sem.at[3 + 2 * t + h],
                )
            )
    ext_column = pl.multiple_of(jnp.where(z - 2 * core == 1, 2 * BLK, 0), BLK)
    local_ext = pltpu.make_async_copy(
        root.at[pl.ds(BLK, BLK), pl.ds(ext_column, BLK)], ext, local_sem.at[7]
    )
    for copy in local:
        copy.start()
    blocks = pltpu.make_async_copy(anc_hbm, anc, local_sem.at[8])
    blocks.start()

    @pl.when(own_diag)
    def _():
        local_ext.start()

    for copy in local:
        copy.wait()

    @pl.when(own_diag)
    def _():
        local_ext.wait()
        for t in range(2):
            rb[t, :, 0:BLK] = rb[t, :, 0:BLK] * jnp.bfloat16(0.5)

    pl.semaphore_wait(barrier, len(partners))

    sent, arrived = {}, set()

    def slots(c, zz, py, lo, hi):
        return pb[c].at[zz, py, pl.ds(core * 3 + lo, hi - lo)]

    def unit(dx, zr, t, lo=0, hi=BLK):
        ref = rb.at[2 * SOURCES.index((dx, zr)) + t]
        return ref if hi - lo == BLK else ref.at[pl.ds(lo, hi - lo)]

    def rows_copy(kind, c):
        m = Z_FIRST[c]
        split = m + FAR_UP[c]
        same = {
            "bu": (slots(c, 0, y, 0, 3), d_yu, ()),
            "bd": (slots(c, 0, y, 0, 3), d_yd, ()),
            "cu": (slots(c, 1, y, 0, m), d_yu, ("a",)),
            "cd": (slots(c, 1, y, 0, m), d_yd, ("a",)),
            "du": (slots(c, 0, down, 0, split), d_yu, ("bu",)),
            "dd": (slots(c, 0, up, split, 3), d_yd, ("bd",)),
            "do": (slots(c, 1, up, 0, m), d_yd, ("cd",)),
            "ka": (pb[c].at[0, :, pl.ds(core * 3, 3)], d_core, ("bu", "bd", "du", "dd")),
            "kb": (pb[c].at[1, :, pl.ds(core * 3, 3)], d_core, ("a", "cu", "cd", "do", "eu", "ed", "ef")),
            "ks": (slots(c, 1, y, 0, 3), d_core, ("a",)),
            "kd": (slots(c, 1, down, 0, 3), d_core, ("cu", "ed")),
            "ku": (slots(c, 1, up, 0, 3), d_core, ("cd", "eu")),
            "kf": (slots(c, 1, far, 0, 3), d_core, ("do", "ef")),
        }
        over = {
            "a": (y, 0, ()),
            "ed": (down, m, ("bu",)),
            "eu": (up, m, ("bd",)),
            "ef": (far, m, ("du", "dd")),
        }
        if kind in same:
            ref, target, first = same[kind]
            return ref, ref, target, first
        py, lo, first = over[kind]
        return slots(c, 0, py, lo, 3), slots(c, 1, py, lo, 3), d_z, first

    half = BLK // 2
    root_copies = {
        "ra0": (unit(0, 0, 0), unit(0, 1, 0), d_zq, ()),
        "ra1": (unit(0, 0, 1), unit(0, 1, 1), d_zq, ()),
        "rb0u": (unit(0, 0, 0), unit(3, 0, 0), d_xu, ()),
        "rb0d": (unit(0, 0, 0), unit(1, 0, 0), d_xd, ()),
        "rb1u": (unit(0, 0, 1), unit(3, 0, 1), d_xu, ()),
        "rb1d": (unit(0, 0, 1), unit(1, 0, 1), d_xd, ()),
        "rc0u": (unit(0, 1, 0), unit(3, 1, 0), d_xu, ("ra0",)),
        "rc0d": (unit(0, 1, 0), unit(1, 1, 0), d_xd, ("ra0",)),
        "rd0u": (unit(3, 0, 0), unit(2, 0, 0), d_xu, ("rb0u",)),
        "rd0d": (unit(1, 1, 0), unit(2, 1, 0), d_xd, ("rc0d",)),
        "rd1u": (unit(3, 0, 1, 0, half), unit(2, 0, 1, 0, half), d_xu, ("rb1u",)),
        "rd1d": (unit(1, 0, 1, half, BLK), unit(2, 0, 1, half, BLK), d_xd, ("rb1d",)),
        "re1d": (unit(3, 0, 1), unit(3, 1, 1), d_zq, ("rb1u",)),
        "re1u": (unit(1, 0, 1), unit(1, 1, 1), d_zq, ("rb1d",)),
        "re1f": (unit(2, 0, 1), unit(2, 1, 1), d_zq, ("rd1u", "rd1d")),
    }

    def arrive(names):
        for name in names:
            if name in sent and name not in arrived:
                sent[name].wait_recv()
                arrived.add(name)

    def send(name):
        if name in root_copies:
            src, dst, target, first = root_copies[name]
        else:
            src, dst, target, first = rows_copy(name[:-1], int(name[-1]))
            first = [kind + name[-1] for kind in first]
        arrive(first)
        n = len(sent)
        sent[name] = pltpu.make_async_remote_copy(
            src_ref=src,
            dst_ref=dst,
            send_sem=send_sem.at[n],
            recv_sem=recv_sem.at[n],
            device_id=target,
            device_id_type=MESH,
        )
        sent[name].start()

    ext_is_mine = z_ext == z
    dx_ext = (x - y + 4) % 4

    def ext_copy(n, target):
        return pltpu.make_async_remote_copy(
            src_ref=ext,
            dst_ref=ext,
            send_sem=ext_send.at[n],
            recv_sem=ext_recv,
            device_id=target,
            device_id_type=MESH,
        )

    to_zq, to_xu, to_xd = ext_copy(0, d_zq), ext_copy(1, d_xu), ext_copy(2, d_xd)
    goes_zq = ext_is_mine
    goes_xu = jnp.logical_and(ext_is_mine, jnp.logical_or(dx_ext == 0, dx_ext == 1))
    goes_xd = jnp.logical_and(ext_is_mine, dx_ext == 0)

    near = jnp.logical_and(ext_is_mine, dx_ext % 2 == 1)
    opposite = jnp.logical_and(ext_is_mine, dx_ext == 2)

    def ext_on(here, more):
        @pl.when(here)
        def _():
            to_zq.wait_recv()

        if more:

            @pl.when(jnp.logical_and(here, dx_ext == 1))
            def _():
                to_xu.start()

        @pl.when(here)
        def _():
            to_zq.start()

    @pl.when(own_diag)
    def _():
        to_xu.start()
        to_xd.start()
        to_zq.start()

    free = next(n for n, name in enumerate(ORDER) if name[0] in "cdekmno")
    for name in ORDER[:free]:
        send(name)

    blocks.wait()
    for c in range(CHILDREN):

        def find(block, at, c=c):
            hit = (anc[c, at] == block).astype(jnp.int32)
            slot_of[c, block] = at
            listed[c, block] = hit.astype(jnp.float32)
            return jnp.minimum(at + hit, MAX_ANC - 1)

        lax.fori_loop(0, ROOT_BLOCKS, find, jnp.int32(0))
    part[...] = jnp.zeros_like(part)
    units = []
    for dx, zr in SOURCES:
        px, pz = (x + dx) % 4, zq if zr else z
        units += [(2 * (px * 4 + pz) + t, window(px, pz, t)) for t in range(2)]

    def build(c):
        for at, key in enumerate((3, 0, 2, 1, 3)):
            block = 4 * q + key
            slot, keep = slot_of[c, block], listed[c, block].astype(jnp.bfloat16)
            for zz in range(2):
                pk[c][at * BLK : (at + 1) * BLK, zz * 128 : (zz + 1) * 128] = (
                    pb[c][zz, slot // 6, slot % 6] * keep
                )

    acc = [[jnp.zeros((8, 128), jnp.float32)] * 2 for _ in range(CHILDREN)]

    def add(c, product, row):
        slot, keep = slot_of[c, row], listed[c, row]
        for zz in range(2):
            mine = pb[c][zz, slot // 6, slot % 6].astype(jnp.float32)
            term = product[:, zz * 128 : (zz + 1) * 128] * mine
            acc[c][zz] = acc[c][zz] + jnp.sum(term.reshape(BLK // 8, 8, 128), axis=0) * keep

    brought = (
        ((), ()),
        (("ra0",), ("ra1",)),
        (("rb0d",), ("rb1d",)),
        (("rb0u",), ("rb1u",)),
        (("rc0d",), ("re1u",)),
        (("rc0u",), ("re1d",)),
        (("rd0u",), ("rd1u", "rd1d")),
        (("rd0d",), ("re1f",)),
    )

    def compute(c, lo, hi):
        for u in range(lo, hi):
            arrive(brought[u // 2][u % 2])
            row, win = units[u]
            start = pl.multiple_of(win * BLK, BLK)
            product = jnp.dot(
                rb[u], pk[c][pl.ds(start, 2 * BLK), :], preferred_element_type=jnp.float32
            )
            add(c, product, row)

    def compute_ext(c):
        start = pl.multiple_of(ext_key * BLK, BLK)
        product = jnp.dot(
            ext[...], pk[c][pl.ds(start, BLK), :], preferred_element_type=jnp.float32
        )
        add(c, product, ext_row)

    def extra():
        @pl.when(jnp.logical_not(ext_is_mine))
        def _():
            to_zq.wait_recv()

        for c in range(CHILDREN - 1):
            compute_ext(c)

    complete = set()
    for name in ORDER[free:]:
        if name == "near":
            ext_on(near, True)
        elif name == "opposite":
            ext_on(opposite, False)
        elif name[0] == "m":
            c, lo, hi = (int(number) for number in name[1:].split(":"))
            if c not in complete:
                if c == CHILDREN - 1:
                    extra()
                arrive([copy for copy in sent if copy[0] != "r" and copy[-1] == str(c)])
                build(c)
                complete.add(c)
            compute(c, lo, hi)
        else:
            send(name)
    compute_ext(CHILDREN - 1)

    for zz in range(2):
        for c in range(CHILDREN):
            part[zz, c : c + 1, :] = 2.0 * jnp.sum(acc[c][zz], axis=0, keepdims=True)
    mine = q * 2 + z % 2
    for g in group:
        pltpu.make_async_remote_copy(
            src_ref=part.at[g[2]],
            dst_ref=red.at[mine],
            send_sem=red_send,
            recv_sem=red_recv,
            device_id=member(*g),
            device_id_type=MESH,
        ).start()
    red[mine] = part[0]
    for copy in sent.values():
        copy.wait_send()

    @pl.when(goes_zq)
    def _():
        to_zq.wait_send()

    @pl.when(goes_xu)
    def _():
        to_xu.wait_send()

    @pl.when(goes_xd)
    def _():
        to_xd.wait_send()

    every = pltpu.make_async_remote_copy(
        src_ref=red.at[pl.ds(0, 15)],
        dst_ref=red.at[pl.ds(0, 15)],
        send_sem=red_send,
        recv_sem=red_recv,
        device_id=d_core,
        device_id_type=MESH,
    )
    every.wait_recv()
    every.wait_send()
    total = red[0]
    for at in range(1, 16):
        total = total + red[at]
    out[...] = total


def per_device(ancestor_blocks, root_inverse, factor_rows, diag_inverse):
    vmem, smem, dma = pltpu.VMEM, pltpu.SMEM, pltpu.SemaphoreType.DMA
    rows = factor_rows.reshape(CHILDREN, 3, BLK, 128)
    total = pl.pallas_call(
        kernel,
        out_shape=vmem((8, 128), jnp.float32),
        in_specs=[
            pl.BlockSpec(memory_space=pl.ANY),
            pl.BlockSpec(memory_space=pl.ANY),
            pl.BlockSpec(memory_space=pl.ANY),
        ],
        out_specs=pl.BlockSpec(memory_space=vmem),
        scratch_shapes=[vmem((2, 4, 6, BLK, 128), jnp.bfloat16)] * CHILDREN
        + [
            vmem((UNITS, BLK, 2 * BLK), jnp.bfloat16),
            vmem((BLK, BLK), jnp.bfloat16),
        ]
        + [vmem((5 * BLK, 2 * 128), jnp.bfloat16)] * CHILDREN
        + [
            vmem((2, 8, 128), jnp.float32),
            vmem((16, 8, 128), jnp.float32),
            smem((CHILDREN, MAX_ANC), jnp.int32),
            smem((CHILDREN, ROOT_BLOCKS), jnp.int32),
            smem((CHILDREN, ROOT_BLOCKS), jnp.float32),
            dma((9,)),
            dma((COPIES,)),
            dma((COPIES,)),
            dma((3,)),
            dma,
            dma,
            dma,
        ],
        compiler_params=pltpu.CompilerParams(
            collective_id=0, has_side_effects=True, vmem_limit_bytes=62 * 2**20
        ),
    )(ancestor_blocks, root_inverse, rows)
    return diag_inverse + total[:CHILDREN]


def solution(mesh):
    in_specs = (P(), P("prow", "pcol"), P(None, "pcol", "prow"), P(None, "prow"))
    out_specs = P(None, "prow")
    return jax.shard_map(
        per_device, mesh=mesh, in_specs=in_specs, out_specs=out_specs, check_vma=False
    )
```

```python
import jax
import jax.numpy as jnp
from jax import lax
from jax.experimental import pallas as pl
from jax.experimental.pallas import tpu as pltpu
from jax.sharding import PartitionSpec as P

MESH = pl.DeviceIdType.MESH
BLK = 256
CHILDREN = 3
ROOT_BLOCKS = 32
MAX_ANC = 24
Z_FIRST = (3, 0, 2)
FAR_UP = (0, 2, 0)
SOURCES = ((0, 0), (0, 1), (1, 0), (3, 0), (1, 1), (3, 1), (2, 0), (2, 1))
UNITS = 2 * len(SOURCES)
ORDER = (
    ("bd1", "bu1", "rb1u", "rb0u", "a0", "bd0", "a2", "rb0d", "bu0", "ra0", "ra1", "eu1", "cd0"),
    ("rb1d", "a1", "du1", "bu2", "bd2", "ed1", "near", "rc0u", "rc0d", "dd1", "du0", "re1d", "rd1u"),
    ("cu0", "do0", "rd1d", "cd2", "re1u", "opposite", "ef1", "ks2", "rd0d", "rd0u", "ka0", "du2", "re1f"),
    ("ka1", "dd2", "eu2", "cu2", "ed2", "kb0", "do2", "kb1", "ef2", "ka2", "m0:8:12", "ku2", "m0:12:14"),
    ("m0:0:8", "m1:12:14", "m1:8:12", "kd2", "kf2", "m1:14:16", "m1:0:8", "m0:14:16", "m2:8:14", "m2:0:8", "m2:14:16"),
)
ORDER = sum(ORDER, ())
COPIES = sum(name[0] in "abcdekr" for name in ORDER)


def pick(index, values):
    out = jnp.int32(values[0])
    for at, value in enumerate(values[1:], 1):
        out = jnp.where(index == at, jnp.int32(value), out)
    return out


def kernel(
    anc_hbm,
    root,
    rows,
    out,
    pb0,
    pb1,
    pb2,
    rb,
    ext,
    pk0,
    pk1,
    pk2,
    part,
    red,
    anc,
    slot_of,
    listed,
    local_sem,
    send_sem,
    recv_sem,
    ext_send,
    ext_recv,
    red_send,
    red_recv,
    ready,
):
    pb, pk = (pb0, pb1, pb2), (pk0, pk1, pk2)
    p, q = lax.axis_index("prow"), lax.axis_index("pcol")
    x, z = p // 4, p % 4
    y, core = q // 2, q % 2
    zp = z + 1 - 2 * (z % 2)
    zq = (z + 3 + 2 * (z % 2)) % 4
    up, down, far = (y + 1) % 4, (y + 3) % 4, (y + 2) % 4

    def device(px, py, pz, pc):
        return (px * 4 + pz, py * 2 + pc)

    d_z = device(x, y, zp, core)
    d_yu, d_yd = device(x, up, z, core), device(x, down, z, core)
    d_zq = device(x, y, zq, core)
    d_xu, d_xd = device((x + 1) % 4, y, z, core), device((x + 3) % 4, y, z, core)
    d_core = device(x, y, z, 1 - core)

    group = [(dy, dc, dz) for dy in (2, 1, 3, 0) for dz in (1, 0) for dc in (1, 0)][:-1]

    def member(dy, dc, dz):
        return device(x, (y + dy) % 4, zp if dz else z, 1 - core if dc else core)

    partners = [d_z, d_yu, d_yd, d_core, d_xu, d_xd]
    tells = z >= 2
    barrier = pltpu.get_barrier_semaphore()
    for partner in partners:
        pl.semaphore_signal(barrier, inc=1, device_id=partner, device_id_type=MESH)

    @pl.when(jnp.logical_not(tells))
    def _():
        pl.semaphore_signal(barrier, inc=1, device_id=d_zq, device_id_type=MESH)

    def window(px, pz, t):
        diagonal = jnp.logical_and(px == y, pz // 2 == core)
        second = pz - 2 * core
        below = px * 4 + pz < 2 * q
        plain = 1 + 2 * jnp.where(below, t, 1 - t)
        special = jnp.where(second == 0, 1, 2) if t == 0 else jnp.where(second == 0, 3, 0)
        return jnp.where(diagonal, special, plain).astype(jnp.int32)

    own_diag = jnp.logical_and(x == y, z // 2 == core)
    z_ext = jnp.where(z // 2 == core, z, zq)
    ext_key = 1 + (z_ext - 2 * core)
    ext_row = 2 * (4 * y + z_ext) + 1

    local = []
    for c in range(CHILDREN):
        local.append(
            pltpu.make_async_copy(
                rows.at[c], pb[c].at[0, y, pl.ds(core * 3, 3)], local_sem.at[c]
            )
        )
    for t in range(2):
        win = window(x, z, t)
        for h, values in enumerate(((3, 0, 2, 1), (0, 2, 1, 3))):
            column = pl.multiple_of(pick(win, values) * BLK, BLK)
            local.append(
                pltpu.make_async_copy(
                    root.at[pl.ds(t * BLK, BLK), pl.ds(column, BLK)],
                    rb.at[t, :, pl.ds(h * BLK, BLK)],
                    local_sem.at[3 + 2 * t + h],
                )
            )
    ext_column = pl.multiple_of(jnp.where(z - 2 * core == 1, 2 * BLK, 0), BLK)
    local_ext = pltpu.make_async_copy(
        root.at[pl.ds(BLK, BLK), pl.ds(ext_column, BLK)], ext, local_sem.at[7]
    )
    for copy in local:
        copy.start()
    blocks = pltpu.make_async_copy(anc_hbm, anc, local_sem.at[8])
    blocks.start()

    @pl.when(own_diag)
    def _():
        local_ext.start()

    for copy in local:
        copy.wait()

    @pl.when(own_diag)
    def _():
        local_ext.wait()
        for t in range(2):
            rb[t, :, 0:BLK] = rb[t, :, 0:BLK] * jnp.bfloat16(0.5)

    pl.semaphore_wait(barrier, len(partners) + tells.astype(jnp.int32))

    @pl.when(tells)
    def _():
        pl.semaphore_signal(ready, inc=1, device_id=d_zq, device_id_type=MESH)

    sent, arrived = {}, set()

    def slots(c, zz, py, lo, hi):
        return pb[c].at[zz, py, pl.ds(core * 3 + lo, hi - lo)]

    def unit(dx, zr, t, lo=0, hi=BLK):
        ref = rb.at[2 * SOURCES.index((dx, zr)) + t]
        return ref if hi - lo == BLK else ref.at[pl.ds(lo, hi - lo)]

    def rows_copy(kind, c):
        m = Z_FIRST[c]
        split = m + FAR_UP[c]
        same = {
            "bu": (slots(c, 0, y, 0, 3), d_yu, ()),
            "bd": (slots(c, 0, y, 0, 3), d_yd, ()),
            "cu": (slots(c, 1, y, 0, m), d_yu, ("a",)),
            "cd": (slots(c, 1, y, 0, m), d_yd, ("a",)),
            "du": (slots(c, 0, down, 0, split), d_yu, ("bu",)),
            "dd": (slots(c, 0, up, split, 3), d_yd, ("bd",)),
            "do": (slots(c, 1, up, 0, m), d_yd, ("cd",)),
            "ka": (pb[c].at[0, :, pl.ds(core * 3, 3)], d_core, ("bu", "bd", "du", "dd")),
            "kb": (pb[c].at[1, :, pl.ds(core * 3, 3)], d_core, ("a", "cu", "cd", "do", "eu", "ed", "ef")),
            "ks": (slots(c, 1, y, 0, 3), d_core, ("a",)),
            "kd": (slots(c, 1, down, 0, 3), d_core, ("cu", "ed")),
            "ku": (slots(c, 1, up, 0, 3), d_core, ("cd", "eu")),
            "kf": (slots(c, 1, far, 0, 3), d_core, ("do", "ef")),
        }
        over = {
            "a": (y, 0, ()),
            "ed": (down, m, ("bu",)),
            "eu": (up, m, ("bd",)),
            "ef": (far, m, ("du", "dd")),
        }
        if kind in same:
            ref, target, first = same[kind]
            return ref, ref, target, first
        py, lo, first = over[kind]
        return slots(c, 0, py, lo, 3), slots(c, 1, py, lo, 3), d_z, first

    half = BLK // 2
    root_copies = {
        "ra0": (unit(0, 0, 0), unit(0, 1, 0), d_zq, ()),
        "ra1": (unit(0, 0, 1), unit(0, 1, 1), d_zq, ()),
        "rb0u": (unit(0, 0, 0), unit(3, 0, 0), d_xu, ()),
        "rb0d": (unit(0, 0, 0), unit(1, 0, 0), d_xd, ()),
        "rb1u": (unit(0, 0, 1), unit(3, 0, 1), d_xu, ()),
        "rb1d": (unit(0, 0, 1), unit(1, 0, 1), d_xd, ()),
        "rc0u": (unit(0, 1, 0), unit(3, 1, 0), d_xu, ("ra0",)),
        "rc0d": (unit(0, 1, 0), unit(1, 1, 0), d_xd, ("ra0",)),
        "rd0u": (unit(3, 0, 0), unit(2, 0, 0), d_xu, ("rb0u",)),
        "rd0d": (unit(1, 1, 0), unit(2, 1, 0), d_xd, ("rc0d",)),
        "rd1u": (unit(3, 0, 1, 0, half), unit(2, 0, 1, 0, half), d_xu, ("rb1u",)),
        "rd1d": (unit(1, 0, 1, half, BLK), unit(2, 0, 1, half, BLK), d_xd, ("rb1d",)),
        "re1d": (unit(3, 0, 1), unit(3, 1, 1), d_zq, ("rb1u",)),
        "re1u": (unit(1, 0, 1), unit(1, 1, 1), d_zq, ("rb1d",)),
        "re1f": (unit(2, 0, 1), unit(2, 1, 1), d_zq, ("rd1u", "rd1d")),
    }

    def arrive(names):
        for name in names:
            if name in sent and name not in arrived:
                sent[name].wait_recv()
                arrived.add(name)

    def send(name):
        if name in root_copies:
            src, dst, target, first = root_copies[name]
        else:
            src, dst, target, first = rows_copy(name[:-1], int(name[-1]))
            first = [kind + name[-1] for kind in first]
        arrive(first)
        if target is d_zq and not any(name[:2] == "ra" for name in sent):
            open_zq()
        n = len(sent)
        sent[name] = pltpu.make_async_remote_copy(
            src_ref=src,
            dst_ref=dst,
            send_sem=send_sem.at[n],
            recv_sem=recv_sem.at[n],
            device_id=target,
            device_id_type=MESH,
        )
        sent[name].start()

    ext_is_mine = z_ext == z
    dx_ext = (x - y + 4) % 4

    def ext_copy(n, target):
        return pltpu.make_async_remote_copy(
            src_ref=ext,
            dst_ref=ext,
            send_sem=ext_send.at[n],
            recv_sem=ext_recv,
            device_id=target,
            device_id_type=MESH,
        )

    to_zq, to_xu, to_xd = ext_copy(0, d_zq), ext_copy(1, d_xu), ext_copy(2, d_xd)
    goes_zq = ext_is_mine
    goes_xu = jnp.logical_and(ext_is_mine, jnp.logical_or(dx_ext == 0, dx_ext == 1))
    goes_xd = jnp.logical_and(ext_is_mine, dx_ext == 0)

    near = jnp.logical_and(ext_is_mine, dx_ext % 2 == 1)
    opposite = jnp.logical_and(ext_is_mine, dx_ext == 2)

    def ext_on(here, more):
        @pl.when(here)
        def _():
            to_zq.wait_recv()

        if more:

            @pl.when(jnp.logical_and(here, dx_ext == 1))
            def _():
                to_xu.start()

        @pl.when(here)
        def _():
            to_zq.start()

    @pl.when(own_diag)
    def _():
        to_xu.start()
        to_xd.start()

    def open_zq():
        @pl.when(jnp.logical_not(tells))
        def _():
            pl.semaphore_wait(ready, 1)

        @pl.when(own_diag)
        def _():
            to_zq.start()

    free = next(n for n, name in enumerate(ORDER) if name[0] in "cdekmno")
    for name in ORDER[:free]:
        send(name)

    blocks.wait()
    for c in range(CHILDREN):

        def find(block, at, c=c):
            hit = (anc[c, at] == block).astype(jnp.int32)
            slot_of[c, block] = at
            listed[c, block] = hit.astype(jnp.float32)
            return jnp.minimum(at + hit, MAX_ANC - 1)

        lax.fori_loop(0, ROOT_BLOCKS, find, jnp.int32(0))
    part[...] = jnp.zeros_like(part)
    units = []
    for dx, zr in SOURCES:
        px, pz = (x + dx) % 4, zq if zr else z
        units += [(2 * (px * 4 + pz) + t, window(px, pz, t)) for t in range(2)]

    def build(c):
        for at, key in enumerate((3, 0, 2, 1, 3)):
            block = 4 * q + key
            slot, keep = slot_of[c, block], listed[c, block].astype(jnp.bfloat16)
            for zz in range(2):
                pk[c][at * BLK : (at + 1) * BLK, zz * 128 : (zz + 1) * 128] = (
                    pb[c][zz, slot // 6, slot % 6] * keep
                )

    acc = [[jnp.zeros((8, 128), jnp.float32)] * 2 for _ in range(CHILDREN)]

    def add(c, product, row):
        slot, keep = slot_of[c, row], listed[c, row]
        for zz in range(2):
            mine = pb[c][zz, slot // 6, slot % 6].astype(jnp.float32)
            term = product[:, zz * 128 : (zz + 1) * 128] * mine
            acc[c][zz] = acc[c][zz] + jnp.sum(term.reshape(BLK // 8, 8, 128), axis=0) * keep

    brought = (
        ((), ()),
        (("ra0",), ("ra1",)),
        (("rb0d",), ("rb1d",)),
        (("rb0u",), ("rb1u",)),
        (("rc0d",), ("re1u",)),
        (("rc0u",), ("re1d",)),
        (("rd0u",), ("rd1u", "rd1d")),
        (("rd0d",), ("re1f",)),
    )

    def compute(c, lo, hi):
        for u in range(lo, hi):
            arrive(brought[u // 2][u % 2])
            row, win = units[u]
            start = pl.multiple_of(win * BLK, BLK)
            product = jnp.dot(
                rb[u], pk[c][pl.ds(start, 2 * BLK), :], preferred_element_type=jnp.float32
            )
            add(c, product, row)

    def compute_ext(c):
        start = pl.multiple_of(ext_key * BLK, BLK)
        product = jnp.dot(
            ext[...], pk[c][pl.ds(start, BLK), :], preferred_element_type=jnp.float32
        )
        add(c, product, ext_row)

    def extra():
        @pl.when(jnp.logical_not(ext_is_mine))
        def _():
            to_zq.wait_recv()

        for c in range(CHILDREN - 1):
            compute_ext(c)

    complete = set()
    for name in ORDER[free:]:
        if name == "near":
            ext_on(near, True)
        elif name == "opposite":
            ext_on(opposite, False)
        elif name[0] == "m":
            c, lo, hi = (int(number) for number in name[1:].split(":"))
            if c not in complete:
                if c == CHILDREN - 1:
                    extra()
                arrive([copy for copy in sent if copy[0] != "r" and copy[-1] == str(c)])
                build(c)
                complete.add(c)
            compute(c, lo, hi)
        else:
            send(name)
    compute_ext(CHILDREN - 1)

    for zz in range(2):
        for c in range(CHILDREN):
            part[zz, c : c + 1, :] = 2.0 * jnp.sum(acc[c][zz], axis=0, keepdims=True)
    mine = q * 2 + z % 2
    for g in group:
        pltpu.make_async_remote_copy(
            src_ref=part.at[g[2]],
            dst_ref=red.at[mine],
            send_sem=red_send,
            recv_sem=red_recv,
            device_id=member(*g),
            device_id_type=MESH,
        ).start()
    red[mine] = part[0]
    for copy in sent.values():
        copy.wait_send()

    @pl.when(goes_zq)
    def _():
        to_zq.wait_send()

    @pl.when(goes_xu)
    def _():
        to_xu.wait_send()

    @pl.when(goes_xd)
    def _():
        to_xd.wait_send()

    every = pltpu.make_async_remote_copy(
        src_ref=red.at[pl.ds(0, 15)],
        dst_ref=red.at[pl.ds(0, 15)],
        send_sem=red_send,
        recv_sem=red_recv,
        device_id=d_core,
        device_id_type=MESH,
    )
    every.wait_recv()
    every.wait_send()
    total = red[0]
    for at in range(1, 16):
        total = total + red[at]
    out[...] = total


def per_device(ancestor_blocks, root_inverse, factor_rows, diag_inverse):
    vmem, smem, dma = pltpu.VMEM, pltpu.SMEM, pltpu.SemaphoreType.DMA
    rows = factor_rows.reshape(CHILDREN, 3, BLK, 128)
    total = pl.pallas_call(
        kernel,
        out_shape=vmem((8, 128), jnp.float32),
        in_specs=[
            pl.BlockSpec(memory_space=pl.ANY),
            pl.BlockSpec(memory_space=pl.ANY),
            pl.BlockSpec(memory_space=pl.ANY),
        ],
        out_specs=pl.BlockSpec(memory_space=vmem),
        scratch_shapes=[vmem((2, 4, 6, BLK, 128), jnp.bfloat16)] * CHILDREN
        + [
            vmem((UNITS, BLK, 2 * BLK), jnp.bfloat16),
            vmem((BLK, BLK), jnp.bfloat16),
        ]
        + [vmem((5 * BLK, 2 * 128), jnp.bfloat16)] * CHILDREN
        + [
            vmem((2, 8, 128), jnp.float32),
            vmem((16, 8, 128), jnp.float32),
            smem((CHILDREN, MAX_ANC), jnp.int32),
            smem((CHILDREN, ROOT_BLOCKS), jnp.int32),
            smem((CHILDREN, ROOT_BLOCKS), jnp.float32),
            dma((9,)),
            dma((COPIES,)),
            dma((COPIES,)),
            dma((3,)),
            dma,
            dma,
            dma,
            pltpu.SemaphoreType.REGULAR,
        ],
        compiler_params=pltpu.CompilerParams(
            collective_id=0, has_side_effects=True, vmem_limit_bytes=62 * 2**20
        ),
    )(ancestor_blocks, root_inverse, rows)
    return diag_inverse + total[:CHILDREN]


def solution(mesh):
    in_specs = (P(), P("prow", "pcol"), P(None, "pcol", "prow"), P(None, "prow"))
    out_specs = P(None, "prow")
    return jax.shard_map(
        per_device, mesh=mesh, in_specs=in_specs, out_specs=out_specs, check_vma=False
    )
```

```python
import jax
import jax.numpy as jnp
from jax import lax
from jax.experimental import pallas as pl
from jax.experimental.pallas import tpu as pltpu
from jax.sharding import PartitionSpec as P

MESH = pl.DeviceIdType.MESH
BLK = 256
CHILDREN = 3
ROOT_BLOCKS = 32
MAX_ANC = 24
Z_FIRST = (3, 0, 2)
FAR_UP = (0, 2, 0)
SOURCES = ((0, 0), (0, 1), (1, 0), (3, 0), (1, 1), (3, 1), (2, 0), (2, 1))
UNITS = 2 * len(SOURCES)
ORDER = (
    ("bd1", "bu1", "rb1u", "rb0u", "a0", "bd0", "a2", "rb0d", "bu0", "ra0", "ra1", "eu1", "cd0"),
    ("rb1d", "a1", "du1", "bu2", "bd2", "ed1", "near", "rc0u", "rc0d", "dd1", "du0", "re1d", "rd1u"),
    ("cu0", "do0", "rd1d", "cd2", "re1u", "opposite", "ef1", "ks2", "rd0d", "rd0u", "ka0", "du2", "re1f"),
    ("ka1", "dd2", "eu2", "cu2", "ed2", "kb0", "do2", "kb1", "ef2", "ka2", "m0:8:12", "ku2", "m0:12:14"),
    ("m0:0:8", "m1:12:14", "m1:8:12", "kd2", "kf2", "m1:14:16", "m1:0:8", "m0:14:16", "m2:8:14", "m2:0:8", "m2:14:16"),
)
ORDER = sum(ORDER, ())
COPIES = sum(name[0] in "abcdekr" for name in ORDER)


def pick(index, values):
    out = jnp.int32(values[0])
    for at, value in enumerate(values[1:], 1):
        out = jnp.where(index == at, jnp.int32(value), out)
    return out


def kernel(
    anc_hbm,
    root,
    rows,
    out,
    pb00,
    pb01,
    pb10,
    pb11,
    pb20,
    pb21,
    rb,
    ext,
    pk0,
    pk1,
    pk2,
    part,
    red,
    anc,
    slot_of,
    listed,
    local_sem,
    send_sem,
    recv_sem,
    ext_send,
    ext_recv,
    red_send,
    red_recv,
    ready,
):
    pb, pk = ((pb00, pb01), (pb10, pb11), (pb20, pb21)), (pk0, pk1, pk2)
    p, q = lax.axis_index("prow"), lax.axis_index("pcol")
    x, z = p // 4, p % 4
    y, core = q // 2, q % 2
    zp = z + 1 - 2 * (z % 2)
    zq = (z + 3 + 2 * (z % 2)) % 4
    up, down, far = (y + 1) % 4, (y + 3) % 4, (y + 2) % 4

    def device(px, py, pz, pc):
        return (px * 4 + pz, py * 2 + pc)

    d_z = device(x, y, zp, core)
    d_yu, d_yd = device(x, up, z, core), device(x, down, z, core)
    d_zq = device(x, y, zq, core)
    d_xu, d_xd = device((x + 1) % 4, y, z, core), device((x + 3) % 4, y, z, core)
    d_core = device(x, y, z, 1 - core)

    group = [(dy, dc, dz) for dy in (2, 1, 3, 0) for dz in (1, 0) for dc in (1, 0)][:-1]

    def member(dy, dc, dz):
        return device(x, (y + dy) % 4, zp if dz else z, 1 - core if dc else core)

    partners = [d_z, d_yu, d_yd, d_core, d_xu, d_xd]
    tells = z >= 2
    barrier = pltpu.get_barrier_semaphore()
    for partner in partners:
        pl.semaphore_signal(barrier, inc=1, device_id=partner, device_id_type=MESH)

    @pl.when(jnp.logical_not(tells))
    def _():
        pl.semaphore_signal(barrier, inc=1, device_id=d_zq, device_id_type=MESH)

    def window(px, pz, t):
        diagonal = jnp.logical_and(px == y, pz // 2 == core)
        second = pz - 2 * core
        below = px * 4 + pz < 2 * q
        plain = 1 + 2 * jnp.where(below, t, 1 - t)
        special = jnp.where(second == 0, 1, 2) if t == 0 else jnp.where(second == 0, 3, 0)
        return jnp.where(diagonal, special, plain).astype(jnp.int32)

    own_diag = jnp.logical_and(x == y, z // 2 == core)
    z_ext = jnp.where(z // 2 == core, z, zq)
    ext_key = 1 + (z_ext - 2 * core)
    ext_row = 2 * (4 * y + z_ext) + 1

    local = []
    for c in range(CHILDREN):
        local.append(
            pltpu.make_async_copy(
                rows.at[c], pb[c][0].at[y, pl.ds(core * 3, 3)], local_sem.at[c]
            )
        )
    for t in range(2):
        win = window(x, z, t)
        for h, values in enumerate(((3, 0, 2, 1), (0, 2, 1, 3))):
            column = pl.multiple_of(pick(win, values) * BLK, BLK)
            local.append(
                pltpu.make_async_copy(
                    root.at[pl.ds(t * BLK, BLK), pl.ds(column, BLK)],
                    rb.at[t, :, pl.ds(h * BLK, BLK)],
                    local_sem.at[3 + 2 * t + h],
                )
            )
    ext_column = pl.multiple_of(jnp.where(z - 2 * core == 1, 2 * BLK, 0), BLK)
    local_ext = pltpu.make_async_copy(
        root.at[pl.ds(BLK, BLK), pl.ds(ext_column, BLK)], ext, local_sem.at[7]
    )
    for copy in local:
        copy.start()
    blocks = pltpu.make_async_copy(anc_hbm, anc, local_sem.at[8])
    blocks.start()

    @pl.when(own_diag)
    def _():
        local_ext.start()

    for copy in local:
        copy.wait()

    @pl.when(own_diag)
    def _():
        local_ext.wait()
        for t in range(2):
            rb[t, :, 0:BLK] = rb[t, :, 0:BLK] * jnp.bfloat16(0.5)

    pl.semaphore_wait(barrier, len(partners) + tells.astype(jnp.int32))

    @pl.when(tells)
    def _():
        pl.semaphore_signal(ready, inc=1, device_id=d_zq, device_id_type=MESH)

    sent, arrived = {}, set()

    def slots(c, zz, py, lo, hi):
        return pb[c][zz].at[py, pl.ds(core * 3 + lo, hi - lo)]

    def unit(dx, zr, t, lo=0, hi=BLK):
        ref = rb.at[2 * SOURCES.index((dx, zr)) + t]
        return ref if hi - lo == BLK else ref.at[pl.ds(lo, hi - lo)]

    def rows_copy(kind, c):
        m = Z_FIRST[c]
        split = m + FAR_UP[c]
        same = {
            "bu": (slots(c, 0, y, 0, 3), d_yu, ()),
            "bd": (slots(c, 0, y, 0, 3), d_yd, ()),
            "cu": (slots(c, 1, y, 0, m), d_yu, ("a",)),
            "cd": (slots(c, 1, y, 0, m), d_yd, ("a",)),
            "du": (slots(c, 0, down, 0, split), d_yu, ("bu",)),
            "dd": (slots(c, 0, up, split, 3), d_yd, ("bd",)),
            "do": (slots(c, 1, up, 0, m), d_yd, ("cd",)),
            "ka": (pb[c][0].at[:, pl.ds(core * 3, 3)], d_core, ("bu", "bd", "du", "dd")),
            "kb": (pb[c][1].at[:, pl.ds(core * 3, 3)], d_core, ("a", "cu", "cd", "do", "eu", "ed", "ef")),
            "ks": (slots(c, 1, y, 0, 3), d_core, ("a",)),
            "kd": (slots(c, 1, down, 0, 3), d_core, ("cu", "ed")),
            "ku": (slots(c, 1, up, 0, 3), d_core, ("cd", "eu")),
            "kf": (slots(c, 1, far, 0, 3), d_core, ("do", "ef")),
        }
        over = {
            "a": (y, 0, ()),
            "ed": (down, m, ("bu",)),
            "eu": (up, m, ("bd",)),
            "ef": (far, m, ("du", "dd")),
        }
        if kind in same:
            ref, target, first = same[kind]
            return ref, ref, target, first
        py, lo, first = over[kind]
        return slots(c, 0, py, lo, 3), slots(c, 1, py, lo, 3), d_z, first

    half = BLK // 2
    root_copies = {
        "ra0": (unit(0, 0, 0), unit(0, 1, 0), d_zq, ()),
        "ra1": (unit(0, 0, 1), unit(0, 1, 1), d_zq, ()),
        "rb0u": (unit(0, 0, 0), unit(3, 0, 0), d_xu, ()),
        "rb0d": (unit(0, 0, 0), unit(1, 0, 0), d_xd, ()),
        "rb1u": (unit(0, 0, 1), unit(3, 0, 1), d_xu, ()),
        "rb1d": (unit(0, 0, 1), unit(1, 0, 1), d_xd, ()),
        "rc0u": (unit(0, 1, 0), unit(3, 1, 0), d_xu, ("ra0",)),
        "rc0d": (unit(0, 1, 0), unit(1, 1, 0), d_xd, ("ra0",)),
        "rd0u": (unit(3, 0, 0), unit(2, 0, 0), d_xu, ("rb0u",)),
        "rd0d": (unit(1, 1, 0), unit(2, 1, 0), d_xd, ("rc0d",)),
        "rd1u": (unit(3, 0, 1, 0, half), unit(2, 0, 1, 0, half), d_xu, ("rb1u",)),
        "rd1d": (unit(1, 0, 1, half, BLK), unit(2, 0, 1, half, BLK), d_xd, ("rb1d",)),
        "re1d": (unit(3, 0, 1), unit(3, 1, 1), d_zq, ("rb1u",)),
        "re1u": (unit(1, 0, 1), unit(1, 1, 1), d_zq, ("rb1d",)),
        "re1f": (unit(2, 0, 1), unit(2, 1, 1), d_zq, ("rd1u", "rd1d")),
    }

    def arrive(names):
        for name in names:
            if name in sent and name not in arrived:
                sent[name].wait_recv()
                arrived.add(name)

    def send(name):
        if name in root_copies:
            src, dst, target, first = root_copies[name]
        else:
            src, dst, target, first = rows_copy(name[:-1], int(name[-1]))
            first = [kind + name[-1] for kind in first]
        arrive(first)
        if target is d_zq and not any(name[:2] == "ra" for name in sent):
            open_zq()
        n = len(sent)
        sent[name] = pltpu.make_async_remote_copy(
            src_ref=src,
            dst_ref=dst,
            send_sem=send_sem.at[n],
            recv_sem=recv_sem.at[n],
            device_id=target,
            device_id_type=MESH,
        )
        sent[name].start()

    ext_is_mine = z_ext == z
    dx_ext = (x - y + 4) % 4

    def ext_copy(n, target):
        return pltpu.make_async_remote_copy(
            src_ref=ext,
            dst_ref=ext,
            send_sem=ext_send.at[n],
            recv_sem=ext_recv,
            device_id=target,
            device_id_type=MESH,
        )

    to_zq, to_xu, to_xd = ext_copy(0, d_zq), ext_copy(1, d_xu), ext_copy(2, d_xd)
    goes_zq = ext_is_mine
    goes_xu = jnp.logical_and(ext_is_mine, jnp.logical_or(dx_ext == 0, dx_ext == 1))
    goes_xd = jnp.logical_and(ext_is_mine, dx_ext == 0)

    near = jnp.logical_and(ext_is_mine, dx_ext % 2 == 1)
    opposite = jnp.logical_and(ext_is_mine, dx_ext == 2)

    def ext_on(here, more):
        @pl.when(here)
        def _():
            to_zq.wait_recv()

        if more:

            @pl.when(jnp.logical_and(here, dx_ext == 1))
            def _():
                to_xu.start()

        @pl.when(here)
        def _():
            to_zq.start()

    @pl.when(own_diag)
    def _():
        to_xu.start()
        to_xd.start()

    def open_zq():
        @pl.when(jnp.logical_not(tells))
        def _():
            pl.semaphore_wait(ready, 1)

        @pl.when(own_diag)
        def _():
            to_zq.start()

    free = next(n for n, name in enumerate(ORDER) if name[0] in "cdekmno")
    for name in ORDER[:free]:
        send(name)

    blocks.wait()
    for c in range(CHILDREN):

        def find(block, at, c=c):
            hit = (anc[c, at] == block).astype(jnp.int32)
            slot_of[c, block] = at
            listed[c, block] = hit.astype(jnp.float32)
            return jnp.minimum(at + hit, MAX_ANC - 1)

        lax.fori_loop(0, ROOT_BLOCKS, find, jnp.int32(0))
    part[...] = jnp.zeros_like(part)
    units = []
    for dx, zr in SOURCES:
        px, pz = (x + dx) % 4, zq if zr else z
        units += [(2 * (px * 4 + pz) + t, window(px, pz, t)) for t in range(2)]

    def build(c, halves=(0, 1)):
        for at, key in enumerate((3, 0, 2, 1, 3)):
            block = 4 * q + key
            slot, keep = slot_of[c, block], listed[c, block].astype(jnp.bfloat16)
            for zz in halves:
                pk[c][at * BLK : (at + 1) * BLK, zz * 128 : (zz + 1) * 128] = (
                    pb[c][zz][slot // 6, slot % 6] * keep
                )

    acc = [[jnp.zeros((8, 128), jnp.float32)] * 2 for _ in range(CHILDREN)]

    def add(c, product, row):
        slot, keep = slot_of[c, row], listed[c, row]
        for zz in range(2):
            mine = pb[c][zz][slot // 6, slot % 6].astype(jnp.float32)
            term = product[:, zz * 128 : (zz + 1) * 128] * mine
            acc[c][zz] = acc[c][zz] + jnp.sum(term.reshape(BLK // 8, 8, 128), axis=0) * keep

    brought = (
        ((), ()),
        (("ra0",), ("ra1",)),
        (("rb0d",), ("rb1d",)),
        (("rb0u",), ("rb1u",)),
        (("rc0d",), ("re1u",)),
        (("rc0u",), ("re1d",)),
        (("rd0u",), ("rd1u", "rd1d")),
        (("rd0d",), ("re1f",)),
    )

    def compute(c, lo, hi):
        for u in range(lo, hi):
            arrive(brought[u // 2][u % 2])
            row, win = units[u]
            start = pl.multiple_of(win * BLK, BLK)
            product = jnp.dot(
                rb[u], pk[c][pl.ds(start, 2 * BLK), :], preferred_element_type=jnp.float32
            )
            add(c, product, row)

    def compute_ext(c):
        start = pl.multiple_of(ext_key * BLK, BLK)
        product = jnp.dot(
            ext[...], pk[c][pl.ds(start, BLK), :], preferred_element_type=jnp.float32
        )
        add(c, product, ext_row)

    def extra():
        @pl.when(jnp.logical_not(ext_is_mine))
        def _():
            to_zq.wait_recv()

        for c in range(CHILDREN - 1):
            compute_ext(c)

    complete = set()
    for name in ORDER[free:]:
        if name == "near":
            ext_on(near, True)
        elif name == "opposite":
            ext_on(opposite, False)
        elif name[0] == "m":
            c, lo, hi = (int(number) for number in name[1:].split(":"))
            if c not in complete:
                mine = [copy for copy in sent if copy[0] != "r" and copy[-1] == str(c)]
                if c == CHILDREN - 1:
                    arrive([copy for copy in mine if copy[:2] in ("bu", "bd", "du", "dd", "ka")])
                    build(c, (0,))
                    extra()
                arrive(mine)
                build(c, (1,) if c == CHILDREN - 1 else (0, 1))
                complete.add(c)
            compute(c, lo, hi)
        else:
            send(name)
    compute_ext(CHILDREN - 1)

    for zz in range(2):
        for c in range(CHILDREN):
            part[zz, c : c + 1, :] = 2.0 * jnp.sum(acc[c][zz], axis=0, keepdims=True)
    mine = q * 2 + z % 2
    for g in group:
        pltpu.make_async_remote_copy(
            src_ref=part.at[g[2]],
            dst_ref=red.at[mine],
            send_sem=red_send,
            recv_sem=red_recv,
            device_id=member(*g),
            device_id_type=MESH,
        ).start()
    red[mine] = part[0]
    for copy in sent.values():
        copy.wait_send()

    @pl.when(goes_zq)
    def _():
        to_zq.wait_send()

    @pl.when(goes_xu)
    def _():
        to_xu.wait_send()

    @pl.when(goes_xd)
    def _():
        to_xd.wait_send()

    every = pltpu.make_async_remote_copy(
        src_ref=red.at[pl.ds(0, 15)],
        dst_ref=red.at[pl.ds(0, 15)],
        send_sem=red_send,
        recv_sem=red_recv,
        device_id=d_core,
        device_id_type=MESH,
    )
    every.wait_recv()
    every.wait_send()
    total = red[0]
    for at in range(1, 16):
        total = total + red[at]
    out[...] = total


def per_device(ancestor_blocks, root_inverse, factor_rows, diag_inverse):
    vmem, smem, dma = pltpu.VMEM, pltpu.SMEM, pltpu.SemaphoreType.DMA
    rows = factor_rows.reshape(CHILDREN, 3, BLK, 128)
    total = pl.pallas_call(
        kernel,
        out_shape=vmem((8, 128), jnp.float32),
        in_specs=[
            pl.BlockSpec(memory_space=pl.ANY),
            pl.BlockSpec(memory_space=pl.ANY),
            pl.BlockSpec(memory_space=pl.ANY),
        ],
        out_specs=pl.BlockSpec(memory_space=vmem),
        scratch_shapes=[vmem((4, 6, BLK, 128), jnp.bfloat16)] * (2 * CHILDREN)
        + [
            vmem((UNITS, BLK, 2 * BLK), jnp.bfloat16),
            vmem((BLK, BLK), jnp.bfloat16),
        ]
        + [vmem((5 * BLK, 2 * 128), jnp.bfloat16)] * CHILDREN
        + [
            vmem((2, 8, 128), jnp.float32),
            vmem((16, 8, 128), jnp.float32),
            smem((CHILDREN, MAX_ANC), jnp.int32),
            smem((CHILDREN, ROOT_BLOCKS), jnp.int32),
            smem((CHILDREN, ROOT_BLOCKS), jnp.float32),
            dma((9,)),
            dma((COPIES,)),
            dma((COPIES,)),
            dma((3,)),
            dma,
            dma,
            dma,
            pltpu.SemaphoreType.REGULAR,
        ],
        compiler_params=pltpu.CompilerParams(
            collective_id=0, has_side_effects=True, vmem_limit_bytes=62 * 2**20
        ),
    )(ancestor_blocks, root_inverse, rows)
    return diag_inverse + total[:CHILDREN]


def solution(mesh):
    in_specs = (P(), P("prow", "pcol"), P(None, "pcol", "prow"), P(None, "prow"))
    out_specs = P(None, "prow")
    return jax.shard_map(
        per_device, mesh=mesh, in_specs=in_specs, out_specs=out_specs, check_vma=False
    )
```

```python
import jax
import jax.numpy as jnp
from jax import lax
from jax.experimental import pallas as pl
from jax.experimental.pallas import tpu as pltpu
from jax.sharding import PartitionSpec as P

MESH = pl.DeviceIdType.MESH
BLK = 256
CHILDREN = 3
ROOT_BLOCKS = 32
MAX_ANC = 24
Z_FIRST = (3, 0, 2)
FAR_UP = (0, 2, 0)
SOURCES = ((0, 0), (0, 1), (1, 0), (3, 0), (1, 1), (3, 1), (2, 0), (2, 1))
UNITS = 2 * len(SOURCES)
ORDER = (
    ("bd1", "bu1", "rb1u", "bd0", "rb0u", "a0", "a2", "rb0d", "bu0", "ra0", "ra1", "eu1", "cd0"),
    ("rb1d", "near", "a1", "du1", "bu2", "bd2", "rc0u", "rd1u", "ed1", "rc0d", "dd1", "du0", "re1d"),
    ("cu0", "do0", "rd1d", "cd2", "opposite", "re1u", "du2", "ef1", "ks2", "rd0d", "rd0u", "ka0", "cu2"),
    ("re1f", "ka1", "eu2", "dd2", "ed2", "kb0", "do2", "kb1", "ef2", "ka2", "m0:8:12", "ku2", "m0:12:14"),
    ("m0:0:8", "m1:12:14", "m1:8:12", "kd2", "kf2", "m1:14:16", "m1:0:8", "m0:14:16", "m2:8:14", "m2:0:8", "m2:14:16"),
)
ORDER = sum(ORDER, ())
COPIES = sum(name[0] in "abcdekr" for name in ORDER)


def pick(index, values):
    out = jnp.int32(values[0])
    for at, value in enumerate(values[1:], 1):
        out = jnp.where(index == at, jnp.int32(value), out)
    return out


def kernel(
    anc_hbm,
    root,
    rows,
    out,
    pb00,
    pb01,
    pb10,
    pb11,
    pb20,
    pb21,
    rb,
    ext,
    pk0,
    pk1,
    pk2,
    part,
    red,
    anc,
    slot_of,
    listed,
    local_sem,
    send_sem,
    recv_sem,
    ext_send,
    ext_recv,
    red_send,
    red_recv,
    ready,
):
    pb, pk = ((pb00, pb01), (pb10, pb11), (pb20, pb21)), (pk0, pk1, pk2)
    p, q = lax.axis_index("prow"), lax.axis_index("pcol")
    x, z = p // 4, p % 4
    y, core = q // 2, q % 2
    zp = z + 1 - 2 * (z % 2)
    zq = (z + 3 + 2 * (z % 2)) % 4
    up, down, far = (y + 1) % 4, (y + 3) % 4, (y + 2) % 4

    def device(px, py, pz, pc):
        return (px * 4 + pz, py * 2 + pc)

    d_z = device(x, y, zp, core)
    d_yu, d_yd = device(x, up, z, core), device(x, down, z, core)
    d_zq = device(x, y, zq, core)
    d_xu, d_xd = device((x + 1) % 4, y, z, core), device((x + 3) % 4, y, z, core)
    d_core = device(x, y, z, 1 - core)

    group = [(dy, dc, dz) for dy in (2, 1, 3, 0) for dz in (1, 0) for dc in (1, 0)][:-1]

    def member(dy, dc, dz):
        return device(x, (y + dy) % 4, zp if dz else z, 1 - core if dc else core)

    partners = [d_z, d_yu, d_yd, d_core, d_xu, d_xd]
    tells = z >= 2
    barrier = pltpu.get_barrier_semaphore()
    for partner in partners:
        pl.semaphore_signal(barrier, inc=1, device_id=partner, device_id_type=MESH)

    @pl.when(jnp.logical_not(tells))
    def _():
        pl.semaphore_signal(barrier, inc=1, device_id=d_zq, device_id_type=MESH)

    def window(px, pz, t):
        diagonal = jnp.logical_and(px == y, pz // 2 == core)
        second = pz - 2 * core
        below = px * 4 + pz < 2 * q
        plain = 1 + 2 * jnp.where(below, t, 1 - t)
        special = jnp.where(second == 0, 1, 2) if t == 0 else jnp.where(second == 0, 3, 0)
        return jnp.where(diagonal, special, plain).astype(jnp.int32)

    own_diag = jnp.logical_and(x == y, z // 2 == core)
    z_ext = jnp.where(z // 2 == core, z, zq)
    ext_key = 1 + (z_ext - 2 * core)
    ext_row = 2 * (4 * y + z_ext) + 1

    local = []
    for c in range(CHILDREN):
        local.append(
            pltpu.make_async_copy(
                rows.at[c], pb[c][0].at[y, pl.ds(core * 3, 3)], local_sem.at[c]
            )
        )
    for t in range(2):
        win = window(x, z, t)
        for h, values in enumerate(((3, 0, 2, 1), (0, 2, 1, 3))):
            column = pl.multiple_of(pick(win, values) * BLK, BLK)
            local.append(
                pltpu.make_async_copy(
                    root.at[pl.ds(t * BLK, BLK), pl.ds(column, BLK)],
                    rb.at[t, :, pl.ds(h * BLK, BLK)],
                    local_sem.at[3 + 2 * t + h],
                )
            )
    ext_column = pl.multiple_of(jnp.where(z - 2 * core == 1, 2 * BLK, 0), BLK)
    local_ext = pltpu.make_async_copy(
        root.at[pl.ds(BLK, BLK), pl.ds(ext_column, BLK)], ext, local_sem.at[7]
    )
    for copy in local:
        copy.start()
    blocks = pltpu.make_async_copy(anc_hbm, anc, local_sem.at[8])
    blocks.start()

    @pl.when(own_diag)
    def _():
        local_ext.start()

    for copy in local:
        copy.wait()

    @pl.when(own_diag)
    def _():
        local_ext.wait()
        for t in range(2):
            rb[t, :, 0:BLK] = rb[t, :, 0:BLK] * jnp.bfloat16(0.5)

    pl.semaphore_wait(barrier, len(partners) + tells.astype(jnp.int32))

    @pl.when(tells)
    def _():
        pl.semaphore_signal(ready, inc=1, device_id=d_zq, device_id_type=MESH)

    sent, arrived = {}, set()

    def slots(c, zz, py, lo, hi):
        return pb[c][zz].at[py, pl.ds(core * 3 + lo, hi - lo)]

    def unit(dx, zr, t, lo=0, hi=BLK):
        ref = rb.at[2 * SOURCES.index((dx, zr)) + t]
        return ref if hi - lo == BLK else ref.at[pl.ds(lo, hi - lo)]

    def rows_copy(kind, c):
        m = Z_FIRST[c]
        split = m + FAR_UP[c]
        same = {
            "bu": (slots(c, 0, y, 0, 3), d_yu, ()),
            "bd": (slots(c, 0, y, 0, 3), d_yd, ()),
            "cu": (slots(c, 1, y, 0, m), d_yu, ("a",)),
            "cd": (slots(c, 1, y, 0, m), d_yd, ("a",)),
            "du": (slots(c, 0, down, 0, split), d_yu, ("bu",)),
            "dd": (slots(c, 0, up, split, 3), d_yd, ("bd",)),
            "do": (slots(c, 1, up, 0, m), d_yd, ("cd",)),
            "ka": (pb[c][0].at[:, pl.ds(core * 3, 3)], d_core, ("bu", "bd", "du", "dd")),
            "kb": (pb[c][1].at[:, pl.ds(core * 3, 3)], d_core, ("a", "cu", "cd", "do", "eu", "ed", "ef")),
            "ks": (slots(c, 1, y, 0, 3), d_core, ("a",)),
            "kd": (slots(c, 1, down, 0, 3), d_core, ("cu", "ed")),
            "ku": (slots(c, 1, up, 0, 3), d_core, ("cd", "eu")),
            "kf": (slots(c, 1, far, 0, 3), d_core, ("do", "ef")),
        }
        over = {
            "a": (y, 0, ()),
            "ed": (down, m, ("bu",)),
            "eu": (up, m, ("bd",)),
            "ef": (far, m, ("du", "dd")),
        }
        if kind in same:
            ref, target, first = same[kind]
            return ref, ref, target, first
        py, lo, first = over[kind]
        return slots(c, 0, py, lo, 3), slots(c, 1, py, lo, 3), d_z, first

    half = BLK // 2
    root_copies = {
        "ra0": (unit(0, 0, 0), unit(0, 1, 0), d_zq, ()),
        "ra1": (unit(0, 0, 1), unit(0, 1, 1), d_zq, ()),
        "rb0u": (unit(0, 0, 0), unit(3, 0, 0), d_xu, ()),
        "rb0d": (unit(0, 0, 0), unit(1, 0, 0), d_xd, ()),
        "rb1u": (unit(0, 0, 1), unit(3, 0, 1), d_xu, ()),
        "rb1d": (unit(0, 0, 1), unit(1, 0, 1), d_xd, ()),
        "rc0u": (unit(0, 1, 0), unit(3, 1, 0), d_xu, ("ra0",)),
        "rc0d": (unit(0, 1, 0), unit(1, 1, 0), d_xd, ("ra0",)),
        "rd0u": (unit(3, 0, 0), unit(2, 0, 0), d_xu, ("rb0u",)),
        "rd0d": (unit(1, 1, 0), unit(2, 1, 0), d_xd, ("rc0d",)),
        "rd1u": (unit(3, 0, 1, 0, half), unit(2, 0, 1, 0, half), d_xu, ("rb1u",)),
        "rd1d": (unit(1, 0, 1, half, BLK), unit(2, 0, 1, half, BLK), d_xd, ("rb1d",)),
        "re1d": (unit(3, 0, 1), unit(3, 1, 1), d_zq, ("rb1u",)),
        "re1u": (unit(1, 0, 1), unit(1, 1, 1), d_zq, ("rb1d",)),
        "re1f": (unit(2, 0, 1), unit(2, 1, 1), d_zq, ("rd1u", "rd1d")),
    }

    def arrive(names):
        for name in names:
            if name in sent and name not in arrived:
                sent[name].wait_recv()
                arrived.add(name)

    def send(name):
        if name in root_copies:
            src, dst, target, first = root_copies[name]
        else:
            src, dst, target, first = rows_copy(name[:-1], int(name[-1]))
            first = [kind + name[-1] for kind in first]
        arrive(first)
        if target is d_zq and not any(name[:2] == "ra" for name in sent):
            open_zq()
        n = len(sent)
        sent[name] = pltpu.make_async_remote_copy(
            src_ref=src,
            dst_ref=dst,
            send_sem=send_sem.at[n],
            recv_sem=recv_sem.at[n],
            device_id=target,
            device_id_type=MESH,
        )
        sent[name].start()

    ext_is_mine = z_ext == z
    dx_ext = (x - y + 4) % 4

    def ext_copy(n, target):
        return pltpu.make_async_remote_copy(
            src_ref=ext,
            dst_ref=ext,
            send_sem=ext_send.at[n],
            recv_sem=ext_recv,
            device_id=target,
            device_id_type=MESH,
        )

    to_zq, to_xu, to_xd = ext_copy(0, d_zq), ext_copy(1, d_xu), ext_copy(2, d_xd)
    goes_zq = ext_is_mine
    goes_xu = jnp.logical_and(ext_is_mine, jnp.logical_or(dx_ext == 0, dx_ext == 1))
    goes_xd = jnp.logical_and(ext_is_mine, dx_ext == 0)

    near = jnp.logical_and(ext_is_mine, dx_ext % 2 == 1)
    opposite = jnp.logical_and(ext_is_mine, dx_ext == 2)

    def ext_on(here, more):
        @pl.when(here)
        def _():
            to_zq.wait_recv()

        if more:

            @pl.when(jnp.logical_and(here, dx_ext == 1))
            def _():
                to_xu.start()

        @pl.when(here)
        def _():
            to_zq.start()

    @pl.when(own_diag)
    def _():
        to_xu.start()
        to_xd.start()

    def open_zq():
        @pl.when(jnp.logical_not(tells))
        def _():
            pl.semaphore_wait(ready, 1)

        @pl.when(own_diag)
        def _():
            to_zq.start()

    free = next(n for n, name in enumerate(ORDER) if name[0] in "cdekmno")
    for name in ORDER[:free]:
        send(name)

    blocks.wait()
    for c in range(CHILDREN):

        def find(block, at, c=c):
            hit = (anc[c, at] == block).astype(jnp.int32)
            slot_of[c, block] = at
            listed[c, block] = hit.astype(jnp.float32)
            return jnp.minimum(at + hit, MAX_ANC - 1)

        lax.fori_loop(0, ROOT_BLOCKS, find, jnp.int32(0))
    part[...] = jnp.zeros_like(part)
    units = []
    for dx, zr in SOURCES:
        px, pz = (x + dx) % 4, zq if zr else z
        units += [(2 * (px * 4 + pz) + t, window(px, pz, t)) for t in range(2)]

    def build(c, halves=(0, 1)):
        for at, key in enumerate((3, 0, 2, 1, 3)):
            block = 4 * q + key
            slot, keep = slot_of[c, block], listed[c, block].astype(jnp.bfloat16)
            for zz in halves:
                pk[c][at * BLK : (at + 1) * BLK, zz * 128 : (zz + 1) * 128] = (
                    pb[c][zz][slot // 6, slot % 6] * keep
                )

    acc = [[jnp.zeros((8, 128), jnp.float32)] * 2 for _ in range(CHILDREN)]

    def add(c, product, row):
        slot, keep = slot_of[c, row], listed[c, row]
        for zz in range(2):
            mine = pb[c][zz][slot // 6, slot % 6].astype(jnp.float32)
            term = product[:, zz * 128 : (zz + 1) * 128] * mine
            acc[c][zz] = acc[c][zz] + jnp.sum(term.reshape(BLK // 8, 8, 128), axis=0) * keep

    brought = (
        ((), ()),
        (("ra0",), ("ra1",)),
        (("rb0d",), ("rb1d",)),
        (("rb0u",), ("rb1u",)),
        (("rc0d",), ("re1u",)),
        (("rc0u",), ("re1d",)),
        (("rd0u",), ("rd1u", "rd1d")),
        (("rd0d",), ("re1f",)),
    )

    def compute(c, lo, hi):
        for u in range(lo, hi):
            arrive(brought[u // 2][u % 2])
            row, win = units[u]
            start = pl.multiple_of(win * BLK, BLK)
            product = jnp.dot(
                rb[u], pk[c][pl.ds(start, 2 * BLK), :], preferred_element_type=jnp.float32
            )
            add(c, product, row)

    def compute_ext(c):
        start = pl.multiple_of(ext_key * BLK, BLK)
        product = jnp.dot(
            ext[...], pk[c][pl.ds(start, BLK), :], preferred_element_type=jnp.float32
        )
        add(c, product, ext_row)

    def extra():
        @pl.when(jnp.logical_not(ext_is_mine))
        def _():
            to_zq.wait_recv()

        for c in range(CHILDREN - 1):
            compute_ext(c)

    complete = set()
    for name in ORDER[free:]:
        if name == "near":
            ext_on(near, True)
        elif name == "opposite":
            ext_on(opposite, False)
        elif name[0] == "m":
            c, lo, hi = (int(number) for number in name[1:].split(":"))
            if c not in complete:
                mine = [copy for copy in sent if copy[0] != "r" and copy[-1] == str(c)]
                if c == CHILDREN - 1:
                    arrive([copy for copy in mine if copy[:2] in ("bu", "bd", "du", "dd", "ka")])
                    build(c, (0,))
                    extra()
                arrive(mine)
                build(c, (1,) if c == CHILDREN - 1 else (0, 1))
                complete.add(c)
            compute(c, lo, hi)
        else:
            send(name)
    compute_ext(CHILDREN - 1)

    for zz in range(2):
        for c in range(CHILDREN):
            part[zz, c : c + 1, :] = 2.0 * jnp.sum(acc[c][zz], axis=0, keepdims=True)
    mine = q * 2 + z % 2
    for g in group:
        pltpu.make_async_remote_copy(
            src_ref=part.at[g[2]],
            dst_ref=red.at[mine],
            send_sem=red_send,
            recv_sem=red_recv,
            device_id=member(*g),
            device_id_type=MESH,
        ).start()
    red[mine] = part[0]
    for copy in sent.values():
        copy.wait_send()

    @pl.when(goes_zq)
    def _():
        to_zq.wait_send()

    @pl.when(goes_xu)
    def _():
        to_xu.wait_send()

    @pl.when(goes_xd)
    def _():
        to_xd.wait_send()

    every = pltpu.make_async_remote_copy(
        src_ref=red.at[pl.ds(0, 15)],
        dst_ref=red.at[pl.ds(0, 15)],
        send_sem=red_send,
        recv_sem=red_recv,
        device_id=d_core,
        device_id_type=MESH,
    )
    every.wait_recv()
    every.wait_send()
    total = red[0]
    for at in range(1, 16):
        total = total + red[at]
    out[...] = total


def per_device(ancestor_blocks, root_inverse, factor_rows, diag_inverse):
    vmem, smem, dma = pltpu.VMEM, pltpu.SMEM, pltpu.SemaphoreType.DMA
    rows = factor_rows.reshape(CHILDREN, 3, BLK, 128)
    total = pl.pallas_call(
        kernel,
        out_shape=vmem((8, 128), jnp.float32),
        in_specs=[
            pl.BlockSpec(memory_space=pl.ANY),
            pl.BlockSpec(memory_space=pl.ANY),
            pl.BlockSpec(memory_space=pl.ANY),
        ],
        out_specs=pl.BlockSpec(memory_space=vmem),
        scratch_shapes=[vmem((4, 6, BLK, 128), jnp.bfloat16)] * (2 * CHILDREN)
        + [
            vmem((UNITS, BLK, 2 * BLK), jnp.bfloat16),
            vmem((BLK, BLK), jnp.bfloat16),
        ]
        + [vmem((5 * BLK, 2 * 128), jnp.bfloat16)] * CHILDREN
        + [
            vmem((2, 8, 128), jnp.float32),
            vmem((16, 8, 128), jnp.float32),
            smem((CHILDREN, MAX_ANC), jnp.int32),
            smem((CHILDREN, ROOT_BLOCKS), jnp.int32),
            smem((CHILDREN, ROOT_BLOCKS), jnp.float32),
            dma((9,)),
            dma((COPIES,)),
            dma((COPIES,)),
            dma((3,)),
            dma,
            dma,
            dma,
            pltpu.SemaphoreType.REGULAR,
        ],
        compiler_params=pltpu.CompilerParams(
            collective_id=0, has_side_effects=True, vmem_limit_bytes=62 * 2**20
        ),
    )(ancestor_blocks, root_inverse, rows)
    return diag_inverse + total[:CHILDREN]


def solution(mesh):
    in_specs = (P(), P("prow", "pcol"), P(None, "pcol", "prow"), P(None, "prow"))
    out_specs = P(None, "prow")
    return jax.shard_map(
        per_device, mesh=mesh, in_specs=in_specs, out_specs=out_specs, check_vma=False
    )
```
